32 devices in a mesh: gx: 2 (over x), gy: 4 (over y, core), gz: 4 (over z).
Axes of the slice: x: 2, y: 2, z: 4, core: 2. Of those that a mesh axis runs over, the one named last changes fastest.
Arguments:
- scalar_feat: bfloat16 [32000, 128], P(('gx', 'gy', 'gz')), may hold values from -6 to 6
- vector_feat: bfloat16 [32000, 384], P(('gx', 'gy', 'gz')), may hold values from -6 to 6
- positions: float32 [3, 32000], P(None, ('gx', 'gy', 'gz')), may hold values from 0 to 26, as said below
- message_inner: bfloat16 [128, 128], replicated, may hold values from -0.5 to 0.5
- message_inner_bias: float32 [128], replicated, may hold values from -3 to 3
- message_outer: bfloat16 [128, 384], replicated, may hold values from -0.5 to 0.5
- message_outer_bias: float32 [384], replicated, may hold values from -3 to 3
- radial_weight: bfloat16 [20, 384], replicated, may hold values from -2.5 to 2.5
- radial_bias: float32 [384], replicated, may hold values from -2 to 2
- update_left: bfloat16 [128, 128], replicated, may hold values from -0.5 to 0.5
- update_right: bfloat16 [128, 128], replicated, may hold values from -0.5 to 0.5
- update_inner: bfloat16 [256, 128], replicated, may hold values from -0.375 to 0.375
- update_inner_bias: float32 [128], replicated, may hold values from -3 to 3
- update_outer: bfloat16 [128, 384], replicated, may hold values from -0.5 to 0.5
- update_outer_bias: float32 [384], replicated, may hold values from -3 to 3
- scalar_cotangent: bfloat16 [32000, 128], P(('gx', 'gy', 'gz')), may hold values from -6 to 6
- vector_cotangent: bfloat16 [32000, 384], P(('gx', 'gy', 'gz')), may hold values from -6 to 6
- x_face_rows: int32 [32, 2, 100], P(('gx', 'gy', 'gz')), may hold values from 0 to 999, as said below
- y_face_rows: int32 [32, 2, 120], P(('gx', 'gy', 'gz')), may hold values from 0 to 1199, as said below
- z_face_rows: int32 [32, 2, 144], P(('gx', 'gy', 'gz')), may hold values from 0 to 1439, as said below
- neighbour_table: int32 [15, 32000], P(None, ('gx', 'gy', 'gz')), may hold values from 0 to 1727, as said below
- hub_atoms: int32 [4096], P(('gx', 'gy', 'gz')), may hold values from 0 to 999, as said below
- hub_table: int32 [11, 4096], P(None, ('gx', 'gy', 'gz')), may hold values from 0 to 1727, as said below
- hub_count: int32 [32], P(('gx', 'gy', 'gz')), may hold values from 32 to 128, as said below
Outputs:
- scalar_out: bfloat16 [32000, 128], P(('gx', 'gy', 'gz'))
- vector_out: bfloat16 [32000, 384], P(('gx', 'gy', 'gz'))
- scalar_grad: float32 [32000, 128], P(('gx', 'gy', 'gz'))
- vector_grad: float32 [32000, 384], P(('gx', 'gy', 'gz'))
- positions_grad: float32 [3, 32000], P(None, ('gx', 'gy', 'gz'))
- message_inner_grad: float32 [128, 128], replicated
- message_inner_bias_grad: float32 [128], replicated
- message_outer_grad: float32 [128, 384], replicated
- message_outer_bias_grad: float32 [384], replicated
- radial_weight_grad: float32 [20, 384], replicated
- radial_bias_grad: float32 [384], replicated
- update_left_grad: float32 [128, 128], replicated
- update_right_grad: float32 [128, 128], replicated
- update_inner_grad: float32 [256, 128], replicated
- update_inner_bias_grad: float32 [128], replicated
- update_outer_grad: float32 [128, 384], replicated
- update_outer_bias_grad: float32 [384], replicated
The draws below stay inside these ranges and needn't reach their ends.
Inputs may be any that keep to these rules, and one draw needn't show every extreme that they name: `x_face_rows`: within a cell each own row appears at most once in each list. `y_face_rows`: entries index a cell's own rows and its x halo rows. `z_face_rows`: entries index a cell's own rows, x halo and y halo rows. `neighbour_table`: an atom's 15 entries are distinct and never its own row. `hub_atoms`: the atoms of one cell's hub slots are distinct. `hub_table`: A hub's entries are distinct, never its own row, and never among its neighbour_table entries. `hub_count`: some cell has all 128 slots live. `positions`: coordinates within the owning cell; an atom and each row that lists it as a neighbour lie 2 or more apart.
All inputs are finite; a program needn't handle non-finite values.
Results may differ from the reference program's by a relative error of at most 0.0089.
Values sent between devices are 32-bit elements; how exact they have to be, the bound alone decides.
No kernel may reach another device: no remote copies, remote signals or barrier semaphores. Data moves between devices by JAX's collectives and lax.ppermute only.
A program may use at most 128 MiB of HBM per device.

```python
import math
import jax
import jax.numpy as jnp
import numpy as np
from jax import lax

F = 128
NRBF = 20
G = 10
NB_REG = 15
NB_HUB = 11
HUB_CAP = 128
ATOMS = 32000
N_GX = 2
N_GY = 4
N_GZ = 4


SPACING = 2.6


JITTER = 0.3


def neighbour_offsets():
    codes = np.array([offset_code for offset_code in range(27) if offset_code != 13])
    return np.stack([codes // 9 - 1, codes // 3 % 3 - 1, codes % 3 - 1], axis=1).astype(np.int32)


def extended_slot(inverse_row, along_x, along_y, along_z):
    owned_count = G * G * G
    face_x = G * G
    face_y = G * (G + 2)
    face_z = (G + 2) * (G + 2)
    clip_x = jnp.clip(along_x, 0, G - 1)
    clip_y = jnp.clip(along_y, 0, G - 1)
    clip_z = jnp.clip(along_z, 0, G - 1)
    owned = inverse_row[(clip_x * G + clip_y) * G + clip_z]
    x_part = owned_count + jnp.where(along_x < 0, 0, face_x) + clip_y * G + clip_z
    y_part = owned_count + 2 * face_x + jnp.where(along_y < 0, 0, face_y) + (along_x + 1) * G + clip_z
    z_part = owned_count + 2 * face_x + 2 * face_y + jnp.where(along_z < 0, 0, face_z) + (along_x + 1) * (G + 2) + (along_y + 1)
    outside_x = (along_x < 0) | (along_x >= G)
    outside_y = (along_y < 0) | (along_y >= G)
    outside_z = (along_z < 0) | (along_z >= G)
    result = jnp.where(outside_z, z_part, jnp.where(outside_y, y_part, jnp.where(outside_x, x_part, owned)))
    return result.astype(jnp.int32)


def shuffled(sub_key):
    return jax.random.permutation(sub_key, G * G * G).astype(jnp.int32)


def lattice_plan(key):
    devices_all = N_GX * N_GY * N_GZ
    owned_count = G * G * G
    perms = jax.vmap(shuffled)(jax.random.split(jax.random.fold_in(key, 11), devices_all))
    inverse = jnp.argsort(perms, axis=1, stable=True).astype(jnp.int32)
    scores = jax.random.randint(jax.random.fold_in(key, 12), (devices_all, owned_count, 26), 0, 1 << 20) * 32 + jnp.arange(26, dtype=jnp.int32)
    ranking = jnp.argsort(scores, axis=2, stable=True).astype(jnp.int32)
    drawn_counts = jax.random.randint(jax.random.fold_in(key, 13), (devices_all,), HUB_CAP // 4, HUB_CAP + 1)
    fullest = jax.random.randint(jax.random.fold_in(key, 14), (), 0, devices_all)
    hub_totals = jnp.where(jnp.arange(devices_all) == fullest, HUB_CAP, drawn_counts).astype(jnp.int32)
    hub_slots = jax.vmap(shuffled)(jax.random.split(jax.random.fold_in(key, 15), devices_all))[:, :HUB_CAP]
    return (perms, inverse, ranking, hub_totals, hub_slots)


def neighbour_slots(perms_row, inverse_row, slot_rows, offset_ids):
    sites = perms_row[slot_rows]
    along_x = sites // (G * G)
    along_y = sites // G % G
    along_z = sites % G
    table = jnp.asarray(neighbour_offsets())[offset_ids]
    return extended_slot(inverse_row, along_x[:, None] + table[..., 0], along_y[:, None] + table[..., 1], along_z[:, None] + table[..., 2])


def draw_positions(key, part):
    perms = lattice_plan(key)[0]
    key = jax.random.fold_in(key, 2)
    sites = perms.reshape(-1)
    coords = jnp.stack([sites // (G * G), sites // G % G, sites % G]).astype(jnp.float32)
    jitter = jax.random.uniform(key, coords.shape, jnp.float32, -JITTER, JITTER)
    return (coords + 0.5) * SPACING + jitter


def draw_x_face_rows(key, part):
    inverse = lattice_plan(key)[1]
    key = jax.random.fold_in(key, 3)
    return jnp.stack([inverse[:, :G * G], inverse[:, G * G * (G - 1):]], axis=1).astype(jnp.int32)


def face_y_rows(inverse_row):
    along_x = jnp.repeat(jnp.arange(-1, G + 1, dtype=jnp.int32), G)
    along_z = jnp.tile(jnp.arange(G, dtype=jnp.int32), G + 2)
    lower = extended_slot(inverse_row, along_x, jnp.zeros_like(along_x), along_z)
    upper = extended_slot(inverse_row, along_x, jnp.full_like(along_x, G - 1), along_z)
    return jnp.stack([lower, upper])


def face_z_rows(inverse_row):
    along_x = jnp.repeat(jnp.arange(-1, G + 1, dtype=jnp.int32), G + 2)
    along_y = jnp.tile(jnp.arange(-1, G + 1, dtype=jnp.int32), G + 2)
    lower = extended_slot(inverse_row, along_x, along_y, jnp.zeros_like(along_x))
    upper = extended_slot(inverse_row, along_x, along_y, jnp.full_like(along_x, G - 1))
    return jnp.stack([lower, upper])


def draw_y_face_rows(key, part):
    inverse = lattice_plan(key)[1]
    key = jax.random.fold_in(key, 4)
    return jax.vmap(face_y_rows)(inverse)


def draw_z_face_rows(key, part):
    inverse = lattice_plan(key)[1]
    key = jax.random.fold_in(key, 6)
    return jax.vmap(face_z_rows)(inverse)


def regular_rows(perms_row, inverse_row, ranking_row):
    slots_all = jnp.arange(G * G * G, dtype=jnp.int32)
    return neighbour_slots(perms_row, inverse_row, slots_all, ranking_row[:, :NB_REG])


def hub_rows(perms_row, inverse_row, ranking_row, slot_row):
    return neighbour_slots(perms_row, inverse_row, slot_row, ranking_row[slot_row][:, NB_REG:])


def draw_neighbour_table(key, part):
    perms, inverse, ranking, hub_totals, hub_slots = lattice_plan(key)
    key = jax.random.fold_in(key, 7)
    table = jax.vmap(regular_rows)(perms, inverse, ranking)
    return jnp.transpose(table, (2, 0, 1)).reshape(NB_REG, -1)


def draw_hub_atoms(key, part):
    hub_slots = lattice_plan(key)[4]
    key = jax.random.fold_in(key, 8)
    return hub_slots.reshape(-1)


def draw_hub_table(key, part):
    perms, inverse, ranking, hub_totals, hub_slots = lattice_plan(key)
    key = jax.random.fold_in(key, 9)
    table = jax.vmap(hub_rows)(perms, inverse, ranking, hub_slots)
    return jnp.transpose(table, (2, 0, 1)).reshape(NB_HUB, -1)


def draw_hub_count(key, part):
    hub_totals = lattice_plan(key)[3]
    key = jax.random.fold_in(key, 10)
    return hub_totals


def block_levels(stream_key, dims, cuts, smallest, high):
    def one(position, parts):
        steps = jax.random.uniform(jax.random.fold_in(jax.random.fold_in(stream_key, 6), position), (parts,), jnp.float32, smallest / len(cuts), high / len(cuts))
        return jnp.repeat(jnp.exp(steps), dims[position] // parts).reshape((-1,) + (1,) * (len(dims) - position - 1))

    loudness = one(*cuts[0])
    for cut in cuts[1:]:
        loudness = loudness * one(*cut)
    return loudness


def centred(rng, extent, scale, most, cuts=(), kind=jnp.bfloat16):
    entries = scale * jax.random.normal(rng, extent, jnp.float32)
    if cuts:
        entries = entries * block_levels(rng, extent, cuts, -0.22, 0.18)
    return jnp.clip(entries, -most, most).astype(kind)


def setup_inputs(seed: int = 0) -> dict:
    splits = jax.random.split(jax.random.key(seed), 25)
    scalar_feat = centred(splits[0], (ATOMS, F), 1.0, 6.0, ((0, 32),))
    vector_feat = centred(splits[1], (ATOMS, 3 * F), 1.0, 6.0, ((0, 32),))
    positions = draw_positions(jax.random.fold_in(splits[24], 71), 0)
    message_inner = centred(splits[3], (F, F), F ** -0.5, 0.5)
    message_inner_bias = centred(splits[4], (F,), 0.5, 3.0, (), jnp.float32)
    message_outer = centred(splits[5], (F, 3 * F), F ** -0.5, 0.5)
    message_outer_bias = centred(splits[6], (3 * F,), 0.5, 3.0, (), jnp.float32)
    radial_weight = centred(splits[7], (NRBF, 3 * F), (NRBF // 4) ** -0.5, 2.5)
    radial_bias = centred(splits[8], (3 * F,), 0.3, 2.0, (), jnp.float32)
    update_left = centred(splits[9], (F, F), F ** -0.5, 0.5)
    update_right = centred(splits[10], (F, F), F ** -0.5, 0.5)
    update_inner = centred(splits[11], (2 * F, F), (2 * F) ** -0.5, 0.375)
    update_inner_bias = centred(splits[12], (F,), 0.5, 3.0, (), jnp.float32)
    update_outer = centred(splits[13], (F, 3 * F), F ** -0.5, 0.5)
    update_outer_bias = centred(splits[14], (3 * F,), 0.5, 3.0, (), jnp.float32)
    scalar_cotangent = centred(splits[15], (ATOMS, F), 1.0, 6.0, ((0, 32),))
    vector_cotangent = centred(splits[16], (ATOMS, 3 * F), 1.0, 6.0, ((0, 32),))
    x_face_rows = draw_x_face_rows(jax.random.fold_in(splits[24], 71), 0)
    y_face_rows = draw_y_face_rows(jax.random.fold_in(splits[24], 71), 0)
    z_face_rows = draw_z_face_rows(jax.random.fold_in(splits[24], 71), 0)
    neighbour_table = draw_neighbour_table(jax.random.fold_in(splits[24], 71), 0)
    hub_atoms = draw_hub_atoms(jax.random.fold_in(splits[24], 71), 0)
    hub_table = draw_hub_table(jax.random.fold_in(splits[24], 71), 0)
    hub_count = draw_hub_count(jax.random.fold_in(splits[24], 71), 0)
    return dict(scalar_feat=scalar_feat, vector_feat=vector_feat, positions=positions, message_inner=message_inner, message_inner_bias=message_inner_bias, message_outer=message_outer, message_outer_bias=message_outer_bias, radial_weight=radial_weight, radial_bias=radial_bias, update_left=update_left, update_right=update_right, update_inner=update_inner, update_inner_bias=update_inner_bias, update_outer=update_outer, update_outer_bias=update_outer_bias, scalar_cotangent=scalar_cotangent, vector_cotangent=vector_cotangent, x_face_rows=x_face_rows, y_face_rows=y_face_rows, z_face_rows=z_face_rows, neighbour_table=neighbour_table, hub_atoms=hub_atoms, hub_table=hub_table, hub_count=hub_count)


SPACING = 2.6
CUTOFF = 5.0
HIGH = lax.Precision.HIGHEST

@jax.custom_vjp
def low(v):
    return lax.optimization_barrier(v.astype(jnp.bfloat16)).astype(jnp.float32)

@jax.custom_vjp
def low_back(v):
    return v

def low_keep(v):
    return (low(v), None)

def low_pass(kept, grad):
    return (grad,)

def back_keep(v):
    return (v, None)

def back_low(kept, grad):
    return (low(grad),)
low.defvjp(low_keep, low_pass)
low_back.defvjp(back_keep, back_low)

def exact(left_side, right_side):
    return jnp.dot(left_side, right_side, precision=HIGH, preferred_element_type=jnp.float32)

def pick_rows(table_row, index_rows):
    return table_row[index_rows]

def pick_columns(table_row, index_rows):
    return table_row[:, index_rows]

def extended_tables(x_face_rows, y_face_rows, z_face_rows):
    grid_shape = (N_GX, N_GY, N_GZ)
    cells = N_GX * N_GY * N_GZ
    owned_count = G * G * G
    owners = jnp.arange(cells, dtype=jnp.int32)[:, None] * owned_count + jnp.arange(owned_count, dtype=jnp.int32)[None, :]
    images = jnp.zeros((cells, 3, owned_count), jnp.int32)
    for axis_number, face_rows in ((0, x_face_rows), (1, y_face_rows), (2, z_face_rows)):
        rows_each = face_rows.shape[2]
        picked_owner = jax.vmap(pick_rows)(owners, face_rows)
        picked_image = jax.vmap(pick_columns)(images, face_rows)
        owner_grid = picked_owner.reshape(grid_shape + (2, rows_each))
        image_grid = picked_image.reshape(grid_shape + (3, 2, rows_each))
        step_vector = (jnp.arange(3) == axis_number).astype(jnp.int32)[:, None]
        from_below = jnp.roll(owner_grid[..., 1, :], 1, axis=axis_number).reshape(cells, rows_each)
        from_above = jnp.roll(owner_grid[..., 0, :], -1, axis=axis_number).reshape(cells, rows_each)
        image_below = jnp.roll(image_grid[..., 1, :], 1, axis=axis_number).reshape(cells, 3, rows_each) - step_vector
        image_above = jnp.roll(image_grid[..., 0, :], -1, axis=axis_number).reshape(cells, 3, rows_each) + step_vector
        owners = jnp.concatenate([owners, from_below, from_above], axis=1)
        images = jnp.concatenate([images, image_below, image_above], axis=2)
    return (owners, images)

def reference(scalar_feat, vector_feat, positions, message_inner, message_inner_bias, message_outer, message_outer_bias, radial_weight, radial_bias, update_left, update_right, update_inner, update_inner_bias, update_outer, update_outer_bias, scalar_cotangent, vector_cotangent, x_face_rows, y_face_rows, z_face_rows, neighbour_table, hub_atoms, hub_table, hub_count):
    owners, images = extended_tables(x_face_rows, y_face_rows, z_face_rows)
    owned_count = G * G * G
    feat_width = scalar_feat.shape[1]
    cell_length = G * SPACING
    cells = N_GX * N_GY * N_GZ
    orders = jnp.arange(1, NRBF + 1).astype(jnp.float32)[:, None]
    regular_targets = jnp.tile(jnp.arange(owned_count, dtype=jnp.int32), NB_REG)

    def layer(scalar, vector, places, w_inner, b_inner, w_outer, b_outer, w_radial, b_radial, w_left, w_right, w_up_in, b_up_in, w_up_out, b_up_out):
        hidden = low(jax.nn.silu(exact(scalar, w_inner) + b_inner))
        filters = low(exact(hidden, w_outer) + b_outer)

        def one_cell(cell):
            ext_ids = owners[cell]
            ext_places = places[:, ext_ids] + images[cell].astype(jnp.float32) * cell_length
            ext_filters = filters[ext_ids]
            ext_vector = vector[ext_ids]
            start = (cell * owned_count).astype(jnp.int32)
            hub_start = (cell * HUB_CAP).astype(jnp.int32)
            regular_source = lax.dynamic_slice_in_dim(neighbour_table, start, owned_count, 1).reshape(-1)
            hub_rows = lax.dynamic_slice_in_dim(hub_atoms, hub_start, HUB_CAP, 0)
            hub_source = lax.dynamic_slice_in_dim(hub_table, hub_start, HUB_CAP, 1).reshape(-1)
            live_hubs = (jnp.arange(HUB_CAP) < hub_count[cell]).astype(jnp.float32)
            source = jnp.concatenate([regular_source, hub_source])
            target = jnp.concatenate([regular_targets, jnp.tile(hub_rows, NB_HUB)])
            weight = jnp.concatenate([jnp.ones((NB_REG * owned_count,), jnp.float32), jnp.tile(live_hubs, NB_HUB)])
            offset = ext_places[:, source] - ext_places[:, target]
            distance = jnp.sqrt(lax.optimization_barrier(jnp.sum(offset * offset, axis=0)))
            direction = offset / distance
            phase_arg = orders * (math.pi / CUTOFF) * distance[None, :]
            radial_basis = low(jnp.sin(phase_arg) / distance[None, :])
            cutoff_factor = jnp.where(distance < CUTOFF, 0.5 * (jnp.cos(math.pi / CUTOFF * distance) + 1.0), 0.0)
            edge_filter = (exact(radial_basis.T, w_radial) + b_radial) * cutoff_factor[:, None]
            mixture = ext_filters[source] * edge_filter * weight[:, None]
            neighbour_vec = ext_vector[source].reshape(-1, 3, feat_width)
            vector_part = neighbour_vec * mixture[:, None, :feat_width] + mixture[:, None, 2 * feat_width:] * direction.T[:, :, None]
            delta_scalar = jax.ops.segment_sum(mixture[:, feat_width:2 * feat_width], target, num_segments=owned_count)
            delta_vector = jax.ops.segment_sum(vector_part.reshape(-1, 3 * feat_width), target, num_segments=owned_count)
            state_s = lax.dynamic_slice_in_dim(scalar, start, owned_count, 0) + delta_scalar
            state_v = lax.dynamic_slice_in_dim(vector, start, owned_count, 0) + delta_vector
            low_vector = low(state_v).reshape(owned_count, 3, feat_width)
            left_part = jnp.einsum('acf,fg->acg', low_vector, w_left, precision=HIGH)
            right_part = jnp.einsum('acf,fg->acg', low_vector, w_right, precision=HIGH)
            inner_part = lax.optimization_barrier(jnp.sum(left_part * right_part, axis=1))
            norm_part = jnp.sqrt(lax.optimization_barrier(jnp.sum(right_part * right_part, axis=1)) + 1.0)
            joined = low(jnp.concatenate([state_s, norm_part], axis=1))
            hidden_up = low(jax.nn.silu(exact(joined, w_up_in) + b_up_in))
            amplitude = exact(hidden_up, w_up_out) + b_up_out
            out_scalar = state_s + amplitude[:, feat_width:2 * feat_width] * inner_part + amplitude[:, 2 * feat_width:]
            out_vector = state_v + (amplitude[:, None, :feat_width] * left_part).reshape(owned_count, 3 * feat_width)
            return (out_scalar, out_vector)
        results = lax.map(jax.checkpoint(one_cell), jnp.arange(cells, dtype=jnp.int32))
        return (results[0].reshape(-1, feat_width), results[1].reshape(-1, 3 * feat_width))
    primals = (scalar_feat.astype(jnp.float32), vector_feat.astype(jnp.float32), positions, message_inner.astype(jnp.float32), message_inner_bias, message_outer.astype(jnp.float32), message_outer_bias, radial_weight.astype(jnp.float32), radial_bias, update_left.astype(jnp.float32), update_right.astype(jnp.float32), update_inner.astype(jnp.float32), update_inner_bias, update_outer.astype(jnp.float32), update_outer_bias)
    outputs, pullback = jax.vjp(layer, *primals)
    grads = pullback((scalar_cotangent.astype(jnp.float32), vector_cotangent.astype(jnp.float32)))
    return (outputs[0].astype(jnp.bfloat16), outputs[1].astype(jnp.bfloat16), grads[0], grads[1], grads[2], grads[3], grads[4], grads[5], grads[6], grads[7], grads[8], grads[9], grads[10], grads[11], grads[12], grads[13], grads[14])
```

```python
import functools
import math

import jax
import jax.numpy as jnp
from jax import lax
from jax.experimental import pallas as pl
from jax.experimental.pallas import tpu as pltpu
from jax.sharding import PartitionSpec as P

G = 10
SPACING = 2.6
CUTOFF = 5.0

LANES = 128
TILE = 8
STEP = 9
SLOTS = 16
ORDER_ROWS = 24
GROUP = 3
PARTS = 4
MIB = 1024 * 1024
f32 = jnp.float32
bf16 = jnp.bfloat16

NN = ((1,), (0,))
NT = ((1,), (1,))
TN = ((0,), (0,))


def up_to(count, step):
    return -(-count // step) * step


def mm(left_side, right_side, dims=NN):
    return lax.dot_general(
        left_side, right_side, (dims, ((), ())), preferred_element_type=f32
    )


def halves(x):
    high = x.astype(bf16)
    return high, (x - high.astype(f32)).astype(bf16)


def thirds(x):
    high = x.astype(bf16)
    rest = x - high.astype(f32)
    middle = rest.astype(bf16)
    return high, middle, (rest - middle.astype(f32)).astype(bf16)


def pick_exact(values, onehot):
    stacked = jnp.concatenate([x.astype(f32) for x in thirds(values)], axis=0).astype(bf16)
    moved = mm(stacked, onehot, NT)
    return (moved[0:TILE] + moved[TILE : 2 * TILE]) + moved[2 * TILE :]


def packed_rows(count):
    return up_to(count + -(-count // LANES), TILE)


def iota(shape, dim):
    return lax.broadcasted_iota(jnp.int32, shape, dim)


def read_places(ref, count):
    pieces = []
    sub = iota((TILE, LANES), 0)
    for part in range(-(-count // LANES)):
        row = count + part
        rows = [
            jnp.broadcast_to(ref[row : row + 1, c * LANES : (c + 1) * LANES], (TILE, LANES))
            for c in range(3)
        ]
        pieces.append(
            jnp.where(sub == 0, rows[0], jnp.where(sub == 1, rows[1], jnp.where(sub == 2, rows[2], 0.0)))
        )
    return pieces[0] if len(pieces) == 1 else jnp.concatenate(pieces, axis=1)


def write_places(ref, count, places):
    width = places.shape[1]
    for part in range(-(-count // LANES)):
        size = min(LANES, width - part * LANES)
        for c in range(3):
            ref[count + part : count + part + 1, c * LANES : c * LANES + size] = places[
                c : c + 1, part * LANES : part * LANES + size
            ]


def shifted_places(ref, count, axis_number, amount):
    places = read_places(ref, count)
    sub = iota(places.shape, 0)
    return places + jnp.where(sub == axis_number, amount, 0.0)


def pair_views(refs, rows):
    if len(refs) == 2:
        return list(refs)
    return [refs[0].at[pl.ds(0, rows)], refs[0].at[pl.ds(rows, rows)]]


def arrived_views(counts, shapes, refs):
    views = []
    at = 0
    for count, size in zip(counts, shapes):
        pair = pair_views(refs[at : at + size], packed_rows(count))
        views += pair if size == 2 else pair[::-1]
        at += size
    return views, refs[at:]


def pack_rows(halo, arrived, list_sc, rows, place, count, out_refs):
    owned = rows.shape[0]
    count8 = up_to(count, TILE)
    columns = list_sc[...].T
    for side, out_ref in enumerate(out_refs):
        column = columns[0:count8, side : side + 1]
        out_ref[...] = jnp.zeros(out_ref.shape, f32)
        onehot = (column == iota((count8, owned), 1).astype(f32)).astype(bf16)
        total = mm(onehot, rows)
        places = pick_exact(place, onehot)
        for (first, size, axis_number, amount), ref in zip(halo, arrived):
            size8 = up_to(size, TILE)
            lane = iota((count8, size8), 1)
            onehot = ((column == (lane + first).astype(f32)) & (lane < size)).astype(bf16)
            total = total + mm(onehot, ref[0:size8, :].astype(bf16))
            arrived_places = shifted_places(ref, size, axis_number, amount)
            places = places + pick_exact(arrived_places[:, 0:size8], onehot)
        out_ref[0:count8, :] = total
        write_places(out_ref, count, places)


def first_pack_kernel(out_size, x_hbm, y_hbm, z_hbm, s_hbm, v_hbm, p_hbm, *rest):
    outs = rest[:out_size]
    (
        rows_ref,
        place_ref,
        y_out,
        z_out,
        x_ref,
        s_ref,
        v_ref,
        p_ref,
        list_sc,
        sems,
    ) = rest[out_size:]
    pairs = (
        (x_hbm, x_ref),
        (s_hbm, s_ref),
        (v_hbm, v_ref),
        (p_hbm, p_ref),
        (y_hbm, y_out),
        (z_hbm, z_out),
    )
    copies = [pltpu.make_async_copy(a, b, sems.at[n]) for n, (a, b) in enumerate(pairs)]
    for copy in copies:
        copy.start()
    count = x_ref.shape[1]
    place_ref[...] = jnp.zeros(place_ref.shape, f32)
    list_sc[...] = jnp.full(list_sc.shape, -1.0, f32)
    for copy in copies:
        copy.wait()
    list_sc[0:2, 0:count] = x_ref[...].astype(f32)
    place_ref[0:3, :] = p_ref[...]
    rows = jnp.concatenate([s_ref[...], v_ref[...]], axis=1)
    out_refs = pair_views(outs, packed_rows(count))
    pack_rows((), (), list_sc, rows, place_ref[...], count, out_refs)
    rows_ref[...] = rows.astype(f32)


def list_to(list_sc, list_ref):
    list_sc[...] = jnp.full(list_sc.shape, -1.0, f32)
    list_sc[0:2, 0 : list_ref.shape[1]] = list_ref[...].astype(f32)


def pack_own_kernel(y_list, z_list, rows_ref, place_ref, *rest):
    outs, list_sc = rest[:4], rest[4]
    rows = rows_ref[...].astype(bf16)
    for n, list_ref in enumerate((y_list, z_list)):
        list_to(list_sc, list_ref)
        pair = outs[2 * n : 2 * n + 2]
        pack_rows((), (), list_sc, rows, place_ref[...], list_ref.shape[1], pair)


def pack_kernel(halo, shapes, out_size, list_ref, own_lower, own_upper, *rest):
    arrived, rest = arrived_views([h[1] for h in halo[::2]], shapes, rest)
    count = list_ref.shape[1]
    count8 = up_to(count, TILE)
    out_refs = pair_views(rest[:out_size], packed_rows(count))
    list_sc = rest[out_size]
    list_to(list_sc, list_ref)
    columns = list_sc[...].T
    sizes = [up_to(h[1], TILE) for h in halo]
    values = jnp.concatenate(
        [ref[0:size, :] for size, ref in zip(sizes, arrived)], axis=0
    ).astype(bf16)
    for side, (own_ref, out_ref) in enumerate(zip((own_lower, own_upper), out_refs)):
        column = columns[0:count8, side : side + 1]
        pieces = []
        places = read_places(own_ref, count)[:, 0:count8]
        for (first, size, axis_number, amount), size8, ref in zip(halo, sizes, arrived):
            lane = iota((count8, size8), 1)
            onehot = ((column == (lane + first).astype(f32)) & (lane < size)).astype(bf16)
            pieces.append(onehot)
            moved = shifted_places(ref, size, axis_number, amount)
            places = places + pick_exact(moved[:, 0:size8], onehot)
        out_ref[...] = own_ref[...]
        total = own_ref[0:count8, :]
        at = 0
        for size8, onehot in zip(sizes, pieces):
            total = total + mm(onehot, values[at : at + size8, :])
            at += size8
        out_ref[0:count8, :] = total
        write_places(out_ref, count, places)


def packet_shapes(axis, count, width, extra):
    rows = packed_rows(count)
    if lax.axis_size(axis) == 2:
        return [jax.ShapeDtypeStruct((2 * rows + extra, width), f32)]
    return [jax.ShapeDtypeStruct((rows + extra, width), f32)] * 2


def first_pack(axis, lists, s, v, p):
    owned, width = s.shape
    count = lists[0].shape[1]
    out = packet_shapes(axis, count, 4 * width, 0)
    far = pl.BlockSpec(memory_space=pltpu.HBM)
    inputs = [pltpu.with_memory_space_constraint(x, pltpu.HBM) for x in (*lists, s, v, p)]
    results = pl.pallas_call(
        functools.partial(first_pack_kernel, len(out)),
        in_specs=[far] * 6,
        out_shape=tuple(out)
        + (
            jax.ShapeDtypeStruct((owned, 4 * width), f32),
            jax.ShapeDtypeStruct((TILE, owned), f32),
        )
        + tuple(jax.ShapeDtypeStruct(x.shape, x.dtype) for x in lists[1:]),
        scratch_shapes=[
            pltpu.VMEM(lists[0].shape, lists[0].dtype),
            pltpu.VMEM(s.shape, s.dtype),
            pltpu.VMEM(v.shape, v.dtype),
            pltpu.VMEM(p.shape, p.dtype),
            pltpu.VMEM((TILE, up_to(count, LANES)), f32),
            pltpu.SemaphoreType.DMA((6,)),
        ],
        compiler_params=pltpu.CompilerParams(vmem_limit_bytes=14 * MIB),
        name="pack_first",
    )(*inputs)
    return list(results[: len(out)]), results[len(out) :]


def pack_own(lists, rows, place):
    shapes = []
    for list_ref in lists:
        shapes += [jax.ShapeDtypeStruct((packed_rows(list_ref.shape[1]), rows.shape[1]), f32)] * 2
    longest = max(list_ref.shape[1] for list_ref in lists)
    return pl.pallas_call(
        pack_own_kernel,
        out_shape=tuple(shapes),
        scratch_shapes=[pltpu.VMEM((TILE, up_to(longest, LANES)), f32)],
        compiler_params=pltpu.CompilerParams(vmem_limit_bytes=14 * MIB),
        name="pack_own",
    )(*lists, rows, place)


def pack_sides(axis, lists, own, halo, shapes, arrived):
    count = lists.shape[1]
    out = packet_shapes(axis, count, own[0].shape[1], 0)
    return pl.pallas_call(
        functools.partial(pack_kernel, tuple(halo), tuple(shapes), len(out)),
        out_shape=tuple(out),
        scratch_shapes=[pltpu.VMEM((TILE, up_to(count, LANES)), f32)],
        compiler_params=pltpu.CompilerParams(vmem_limit_bytes=14 * MIB),
        name="pack_rows",
    )(lists, *own, *arrived)


def build_places(place_sc, p_ref, owned, halo, arrived):
    place_sc[...] = jnp.zeros(place_sc.shape, f32)
    place_sc[:, 0:owned] = p_ref[...]
    for (first, rows, axis_number, amount), ref in zip(halo, arrived):
        places = shifted_places(ref, rows, axis_number, amount)
        place_sc[:, first : first + rows] = places[:, 0:rows]


def order_kernel(
    table_ref,
    hub_table_ref,
    place_ref,
    table_out,
    flat_out,
    hub_out,
    target_out,
    place_out,
    wide_sc,
    stack_sc,
    tall_sc,
):
    listed, owned = table_ref.shape
    slots = wide_sc.shape[1]
    wide_sc[...] = jnp.zeros(wide_sc.shape, jnp.int32)
    wide_sc[0:listed, 0:owned] = table_ref[...]
    lane = iota((1, slots), 1)
    worst = jnp.max(wide_sc[...].astype(f32), axis=0, keepdims=True)
    inner = (worst < owned) & (lane < owned)
    flag = inner.astype(f32)
    before = (iota((slots, slots), 0) <= iota((slots, slots), 1)).astype(bf16)
    count = mm(jnp.broadcast_to(flag, (TILE, slots)).astype(bf16), before)[0:1, :]
    total = count[:, slots - 1 : slots]
    index = lane.astype(f32)
    slot = jnp.where(inner, count - 1.0, total + index - count)
    moved = (iota((slots, slots), 0).astype(f32) == slot).astype(bf16)
    table = wide_sc[...]
    stack_sc[...] = jnp.zeros(stack_sc.shape, f32)
    stack_sc[0:SLOTS] = (table >> 8).astype(f32)
    stack_sc[SLOTS : 2 * SLOTS] = (table & 255).astype(f32)
    stack_sc[32:33] = (lane >> 8).astype(f32)
    stack_sc[33:34] = (lane & 255).astype(f32)
    for n, part in enumerate(thirds(place_ref[...])):
        at = 40 + n * TILE
        stack_sc[at : at + TILE, 0:owned] = part.astype(f32)
    turned = mm(stack_sc[...].astype(bf16), moved, NT)
    sorted_table = turned[0:SLOTS] * 256.0 + turned[SLOTS : 2 * SLOTS]
    table_out[...] = sorted_table.astype(jnp.int32)
    place_out[...] = (turned[40:48] + turned[48:56]) + turned[56:64]
    target = jnp.minimum(turned[32:33] * 256.0 + turned[33:34], owned - 1.0)
    for b in range(slots // LANES):
        part = target[:, b * LANES : (b + 1) * LANES]
        target_out[b : b + 1, :] = part.astype(jnp.int32) * TILE
    target_out[TILE:, :] = jnp.broadcast_to(total, (TILE, LANES)).astype(jnp.int32)

    def in_use_order(values, groups, out_ref):
        tall_sc[...] = jnp.zeros(tall_sc.shape, f32)
        for b in range(values.shape[1] // LANES):
            block = jnp.concatenate(
                [
                    values[:, b * LANES : (b + 1) * LANES],
                    jnp.zeros((LANES - values.shape[0], LANES), f32),
                ],
                axis=0,
            )
            tall_sc[b * LANES : (b + 1) * LANES, :] = block.T * 8.0
        rows = iota((LANES, LANES), 0)
        lanes = iota((LANES, LANES), 1)
        total = None
        for n in range(TILE):
            part = tall_sc[pl.ds(n, groups, TILE), :]
            high = jnp.floor(part * (1.0 / 256.0))
            low = part - high * 256.0
            place = (lanes == rows * TILE + n).astype(bf16)
            value = mm(high.astype(bf16), place) * 256.0 + mm(low.astype(bf16), place)
            total = value if total is None else total + value
        out_ref[...] = total.astype(jnp.int32)

    in_use_order(sorted_table, slots // TILE, flat_out)
    hubs = jnp.concatenate(
        [
            hub_table_ref[...].astype(f32),
            jnp.zeros((SLOTS - hub_table_ref.shape[0], LANES), f32),
        ],
        axis=0,
    )
    in_use_order(hubs, LANES // TILE, hub_out)


def order_atoms(table, hub_table, place):
    slots = up_to(table.shape[1], LANES)
    return pl.pallas_call(
        order_kernel,
        out_shape=(
            jax.ShapeDtypeStruct((SLOTS, slots), jnp.int32),
            jax.ShapeDtypeStruct((slots // TILE, LANES), jnp.int32),
            jax.ShapeDtypeStruct((LANES // TILE, LANES), jnp.int32),
            jax.ShapeDtypeStruct((2 * TILE, LANES), jnp.int32),
            jax.ShapeDtypeStruct((TILE, slots), f32),
        ),
        scratch_shapes=[
            pltpu.VMEM((SLOTS, slots), jnp.int32),
            pltpu.VMEM((64, slots), f32),
            pltpu.VMEM((slots, LANES), f32),
        ],
        compiler_params=pltpu.CompilerParams(vmem_limit_bytes=24 * MIB),
        name="order_atoms",
    )(table, hub_table, place)


def build_radial(wext32, wext, wr_ref, br_ref):
    width = wr_ref.shape[1] // 3
    orders = wr_ref.shape[0]
    wr = wr_ref[...].astype(f32)
    br = br_ref[...]
    bias_high = br.astype(bf16).astype(f32)
    bias_low = br - bias_high
    wext32[...] = jnp.zeros(wext32.shape, f32)
    for block, (row, column) in enumerate(
        ((0, 0), (0, 1), (1, 2), (2, 3), (3, 4))
    ):
        source = min(block, 2)
        at = row * ORDER_ROWS
        lanes = slice(column * width, (column + 1) * width)
        cols = slice(source * width, (source + 1) * width)
        wext32[at : at + orders, lanes] = wr[:, cols]
        wext32[at + orders : at + orders + 1, lanes] = bias_high[:, cols]
        wext32[at + orders + 1 : at + orders + 2, lanes] = bias_low[:, cols]
    wext[...] = wext32[...].astype(bf16)


def load_indices(idx_sc, tpos_sc, table_ref, target_ref):
    blocks = table_ref.shape[1] // LANES
    rows = idx_sc.shape[0]
    for b in range(blocks):
        at = b * SLOTS
        lanes = slice(b * LANES, (b + 1) * LANES)
        idx_sc[at : at + SLOTS, :] = table_ref[:, lanes]
        for c in range(3):
            tpos_sc[c * rows + at : c * rows + at + SLOTS, :] = jnp.broadcast_to(
                target_ref[c : c + 1, lanes], (SLOTS, LANES)
            )


def load_hubs(idx_sc, tpos_sc, hub_table_ref, hub_row_ref, place_sc, owned):
    rows = idx_sc.shape[0]
    at = rows - SLOTS
    idx_sc[at:, :] = jnp.zeros((SLOTS, LANES), jnp.int32)
    idx_sc[at : at + hub_table_ref.shape[0], :] = hub_table_ref[...]
    hub = jnp.broadcast_to(hub_row_ref[...], (TILE, LANES))
    lane = hub & (LANES - 1)
    chunk = hub >> 7
    total = jnp.zeros((TILE, LANES), f32)
    for t in range(-(-owned // LANES)):
        part = jnp.take_along_axis(
            place_sc[:, t * LANES : (t + 1) * LANES], lane, axis=1, mode="promise_in_bounds"
        )
        total = jnp.where(chunk == t, part, total)
    for c in range(3):
        tpos_sc[c * rows + at : c * rows + at + SLOTS, :] = jnp.broadcast_to(
            total[c : c + 1, :], (SLOTS, LANES)
        )


def geometry(idx, target, live, place_sc):
    lane = idx & (LANES - 1)
    chunk = idx >> 7
    chunks = place_sc.shape[1] // LANES
    offsets = []
    for c in range(3):
        total = jnp.zeros(idx.shape, f32)
        for t in range(chunks):
            table = jnp.broadcast_to(place_sc[c : c + 1, t * LANES : (t + 1) * LANES], idx.shape)
            part = jnp.take_along_axis(table, lane, axis=1, mode="promise_in_bounds")
            total = jnp.where(chunk == t, part, total)
        offsets.append(total - target[c])
    square = offsets[0] * offsets[0] + offsets[1] * offsets[1] + offsets[2] * offsets[2]
    distance = jnp.sqrt(jnp.where(live, square, 4.0))
    inverse = 1.0 / distance
    direction = [offset * inverse for offset in offsets]
    angle = (math.pi / CUTOFF) * distance
    sine = jnp.sin(angle)
    cosine = jnp.cos(angle)
    inside = live & (distance < CUTOFF)
    factor = jnp.where(inside, 0.5 * (cosine + 1.0), 0.0)
    slope = jnp.where(inside, (-0.5 * math.pi / CUTOFF) * sine, 0.0)
    return inverse, direction, sine, cosine, factor, slope


def fill_geometry(
    groups, blocks, owned, listed, hub_listed, hub_live, idx_sc, tpos_sc, place_sc, basis_sc, slope_sc, geo_sc, orders
):
    rows = idx_sc.shape[0]
    group = GROUP * SLOTS

    def step(i, carry):
        first = pl.multiple_of(i * group, SLOTS)

        def at(q):
            return pl.ds(pl.multiple_of(q * rows + first, SLOTS), group)

        row = iota((group, LANES), 0) + first
        block = row >> 4
        last = block == blocks
        valid = jnp.where(last, hub_live, owned - block * LANES)
        depth = jnp.where(last, hub_listed, listed)
        live = (iota((group, LANES), 1) < valid) & ((row & (SLOTS - 1)) < depth)
        inverse, direction, sine, cosine, factor, slope = geometry(
            idx_sc[pl.ds(first, group), :], [tpos_sc[at(c), :] for c in range(3)], live, place_sc
        )
        geo_sc[at(0), :] = factor
        for c in range(3):
            geo_sc[at(1 + c), :] = direction[c]
        geo_sc[at(4), :] = slope
        geo_sc[at(5), :] = inverse
        sine_n, cosine_n = sine, cosine
        for n in range(orders):
            ratio = sine_n * inverse
            basis_sc[at(n), :] = ratio.astype(bf16).astype(f32)
            if slope_sc is not None:
                slope_sc[at(n), :] = (((n + 1) * math.pi / CUTOFF) * cosine_n - ratio) * inverse
            if n + 1 < orders:
                sine_n, cosine_n = (
                    sine_n * cosine + cosine_n * sine,
                    cosine_n * cosine - sine_n * sine,
                )
        return carry

    lax.fori_loop(0, groups, step, 0)
    basis_sc[orders * rows : (orders + 2) * rows, :] = jnp.ones((2 * rows, LANES), f32)
    rest = (ORDER_ROWS - orders - 2) * rows
    basis_sc[(orders + 2) * rows :, :] = jnp.zeros((rest, LANES), f32)
    if slope_sc is not None:
        slope_sc[orders * rows :, :] = jnp.zeros((rest + 2 * rows, LANES), f32)


def unrolled(count, most):
    for size in range(most, 0, -1):
        if count % size == 0:
            return size
    return 1


def order_tiles(ref, row, rows):
    return [
        ref[pl.ds(row + t * TILE * rows, TILE, rows), :] for t in range(ORDER_ROWS // TILE)
    ]


def edge_coefficients(b, k, rows, basis_sc, geo_sc):
    row = b * SLOTS + k
    basis = order_tiles(basis_sc, row, rows)
    scale = [geo_sc[pl.ds(row + q * rows, 1), :] for q in range(4)]
    return basis, scale


def scaled_parts(basis, scale):
    plain = [part * scale[0] for part in basis]
    parts = []
    for c in range(3):
        parts += [part * scale[1 + c] for part in plain]
    return plain, parts


def make_filters(b, slots, rows, basis_sc, geo_sc, wext, filt, width):
    weights = wext[...]
    size = unrolled(slots, 5)
    for first in range(0, slots, size):
        turned = []
        for k in range(first, first + size):
            basis, scale = edge_coefficients(b, k, rows, basis_sc, geo_sc)
            plain, parts = scaled_parts(basis, scale)
            turned.append(jnp.concatenate(plain + parts, axis=0).T.astype(bf16))
        store_filters(first, turned, weights, filt, width)


def put_slot(filt, k, slot, value):
    filt[:, pl.ds(k * TILE * STEP + slot, TILE, STEP), :] = value.reshape(-1, TILE, LANES)


def get_slot(filt, k, slot):
    return filt[:, pl.ds(k * TILE * STEP + slot, TILE, STEP), :].reshape(LANES, LANES)


def store_filters(first, coeffs, weights, filt, width):
    product = mm(jnp.concatenate(coeffs, axis=0), weights)
    for n in range(len(coeffs)):
        for slot in range(7):
            column = 0 if slot < 3 else slot - 2
            put_slot(
                filt,
                first + n,
                slot,
                product[n * LANES : (n + 1) * LANES, column * width : (column + 1) * width],
            )


def fill_filters(slots, turned_sc, wext, filt, width, extra):
    weights = wext[...]
    size = unrolled(slots, 5)
    for first in range(0, slots, size):
        coeff = [turned_sc[k * LANES : (k + 1) * LANES, :] for k in range(first, first + size)]
        store_filters(first, coeff, weights, filt, width)
        for k in range(first, first + size):
            put_slot(filt, k, 7, extra(k))


def sigmoid(t):
    return 1.0 / (1.0 + jnp.exp(-t))


def message_net(rows, w1, b1, w2, b2):
    lead = rows[:, 0:LANES].astype(bf16)
    pre = mm(lead, w1) + b1
    gate = sigmoid(pre)
    hidden = (pre * gate).astype(bf16)
    filters = (mm(hidden, w2) + b2).astype(bf16).astype(f32)
    return lead, pre, gate, hidden, filters


def store_table(tiles, firsts, counts, rows, filters):
    gate = filters[:, 0:LANES]
    columns = [rows[:, (1 + c) * LANES : (2 + c) * LANES] * gate for c in range(3)]
    columns += [filters[:, LANES : 2 * LANES]] + [filters[:, 2 * LANES :]] * 3
    at = 0
    for first, count in zip(firsts, counts):
        for slot, column in enumerate(columns):
            tiles[pl.ds(first * TILE + slot, count, TILE), :] = column[at : at + count, :]
        at += count


def build_table(tiles, halo, arrived, w1, b1, w2, b2):
    counts = [up_to(h[1], TILE) for h in halo]
    firsts = [h[0] for h in halo]
    sides = jnp.concatenate([ref[0:count, :] for count, ref in zip(counts, arrived)], axis=0)
    store_table(tiles, firsts, counts, sides, message_net(sides, w1, b1, w2, b2)[4])


def tile_at(ref, row):
    return ref[pl.ds(pl.multiple_of(row * TILE, TILE), TILE), :]


def edge_at(k, n):
    return pl.ds((k * TILE + n) * STEP, TILE)


def source_at(ref, row):
    return ref[pl.ds(pl.multiple_of(row, TILE), TILE), :]


def sum_group(filt, tiles, flat, targets, sums, b, i, listed):
    first = b * LANES + i * TILE
    for n in range(TILE):
        total = None
        for k in range(listed):
            source = flat[first * SLOTS + k * TILE + n]
            part = source_at(tiles, source) * filt[i, edge_at(k, n), :]
            total = part if total is None else total + part
        sums[pl.ds(pl.multiple_of(targets[first + n], TILE), TILE), :] = total


def inner_kernel(
    listed,
    flat,
    targets,
    rows_ref,
    p_ref,
    table_ref,
    target_ref,
    w1_ref,
    b1_ref,
    w2_ref,
    b2_ref,
    wr_ref,
    br_ref,
    sums,
    tiles,
    filt,
    place_sc,
    idx_sc,
    tpos_sc,
    basis_sc,
    geo_sc,
    wext32,
    wext,
):
    owned = rows_ref.shape[0]
    orders = wr_ref.shape[0]
    rows = idx_sc.shape[0]
    place_sc[...] = jnp.zeros(place_sc.shape, f32)
    place_sc[:, 0:owned] = p_ref[...]
    build_radial(wext32, wext, wr_ref, br_ref)
    load_indices(idx_sc, tpos_sc, table_ref, target_ref)
    done = targets[TILE * LANES] // TILE
    each = LANES // TILE
    blocks = (done + each - 1) // each
    fill_geometry(
        (blocks + GROUP - 1) // GROUP,
        rows // SLOTS,
        owned,
        listed,
        0,
        0,
        idx_sc,
        tpos_sc,
        place_sc,
        basis_sc,
        None,
        geo_sc,
        orders,
    )
    own = rows_ref[...]
    weights = (w1_ref[...], b1_ref[...], w2_ref[...], b2_ref[...])
    store_table(tiles, [0], [owned], own, message_net(own, *weights)[4])
    sums[...] = jnp.zeros(sums.shape, f32)

    def regular_block(b, carry):
        make_filters(b, listed, rows, basis_sc, geo_sc, wext, filt, LANES)

        def atoms(i, inner):
            sum_group(filt, tiles, flat, targets, sums, b, i, listed)
            return inner

        lax.fori_loop(0, jnp.minimum(each, done - b * each), atoms, 0)
        return carry

    lax.fori_loop(0, blocks, regular_block, 0)


def forward_kernel(
    halo,
    shapes,
    listed,
    hub_listed,
    chunk,
    size_y,
    flat_table,
    flat_hub_table,
    targets,
    hub_list,
    hub_count,
    place_y,
    rows_ref,
    p_ref,
    cot_ref,
    table_ref,
    target_ref,
    hub_table_ref,
    hub_row_ref,
    sums_in,
    w1_ref,
    b1_ref,
    w2_ref,
    b2_ref,
    wr_ref,
    br_ref,
    u_ref,
    v_ref,
    w3_ref,
    b3_ref,
    w4_ref,
    b4_ref,
    *rest,
):
    arrived, rest = arrived_views([h[1] for h in halo[::2]], shapes, rest)
    (
        out_s_ref,
        out_v_ref,
        grad_ref,
        bias_ref,
        tiles,
        basis_sc,
        slope_sc,
        geo_sc,
    ) = rest[:8]
    share_refs = rest[8 : 8 + size_y]
    (
        filt,
        sums,
        place_sc,
        idx_sc,
        tpos_sc,
        wext32,
        wext,
        uv,
        out_sc,
        early_ref,
    ) = rest[8 + size_y :]
    owned = rows_ref.shape[0]
    width = LANES
    orders = wr_ref.shape[0]
    blocks = -(-owned // LANES)
    build_places(place_sc, p_ref, owned, halo, arrived)
    build_radial(wext32, wext, wr_ref, br_ref)
    load_indices(idx_sc, tpos_sc, table_ref, target_ref)
    load_hubs(idx_sc, tpos_sc, hub_table_ref, hub_row_ref, place_sc, owned)
    hub_live = hub_count[0]
    fill_geometry(
        -(-(blocks + 1) // GROUP), blocks, owned, listed, hub_listed, hub_live, idx_sc, tpos_sc, place_sc, basis_sc, slope_sc, geo_sc, orders
    )
    rows = idx_sc.shape[0]
    sums[...] = sums_in[...]
    weights = (w1_ref[...], b1_ref[...], w2_ref[...], b2_ref[...])
    own = rows_ref[...]
    store_table(tiles, [0], [owned], own, message_net(own, *weights)[4])
    build_table(tiles, halo, arrived, *weights)
    done = targets[TILE * LANES] // TILE
    each = LANES // TILE

    def regular_block(b, carry):
        make_filters(b, listed, rows, basis_sc, geo_sc, wext, filt, width)

        def atoms(i, inner):
            sum_group(filt, tiles, flat_table, targets, sums, b, i, listed)
            return inner

        start = jnp.maximum(done - b * each, 0)
        lax.fori_loop(start, jnp.minimum(each, owned // TILE - b * each), atoms, 0)
        return carry

    lax.fori_loop(done // each, blocks, regular_block, 0)
    hub_span = min(listed, up_to(hub_listed, 4))
    make_filters(blocks, hub_span, rows, basis_sc, geo_sc, wext, filt, width)

    def hub_slots(i, carry):
        for n in range(TILE):
            total = None
            for k in range(hub_listed):
                source = flat_hub_table[i * LANES + k * TILE + n]
                part = source_at(tiles, source) * filt[i, edge_at(k, n), :]
                total = part if total is None else total + part
            at = pl.ds(pl.multiple_of(hub_list[i * TILE + n] * TILE, TILE), TILE)
            sums[at, :] = sums[at, :] + total
        return carry

    lax.fori_loop(0, (hub_live + TILE - 1) // TILE, hub_slots, 0)

    uv[:, 0:width] = u_ref[...]
    uv[:, width:] = v_ref[...]
    early_ref[...] = jnp.zeros(early_ref.shape, f32)
    bias_ref[...] = jnp.zeros(bias_ref.shape, f32)

    def update(i, carry):
        first = pl.multiple_of(i * chunk, TILE)
        part = [sums[pl.ds(first * TILE + slot, chunk, TILE), :] for slot in range(7)]
        own = rows_ref[pl.ds(first, chunk), :]
        cot = cot_ref[pl.ds(first, chunk), :]
        state_s = own[:, 0:width] + part[3]
        state_v = [
            own[:, (1 + c) * width : (2 + c) * width] + (part[c] + part[4 + c]) for c in range(3)
        ]
        low = [x.astype(bf16) for x in state_v]
        both = [mm(x, uv[...]) for x in low]
        left = [x[:, 0:width] for x in both]
        right = [x[:, width:] for x in both]
        inner = left[0] * right[0] + left[1] * right[1] + left[2] * right[2]
        norm = jnp.sqrt(right[0] * right[0] + right[1] * right[1] + right[2] * right[2] + 1.0)
        joined = jnp.concatenate([state_s, norm], axis=1).astype(bf16)
        pre = mm(joined, w3_ref[...]) + b3_ref[...]
        gate = sigmoid(pre)
        hidden = (pre * gate).astype(bf16)
        amp = mm(hidden, w4_ref[...]) + b4_ref[...]
        amp_vv = amp[:, 0:width]
        amp_sv = amp[:, width : 2 * width]
        amp_ss = amp[:, 2 * width :]
        out_sc[pl.ds(first, chunk), 0:width] = state_s + amp_sv * inner + amp_ss
        for c in range(3):
            out_sc[pl.ds(first, chunk), (1 + c) * width : (2 + c) * width] = (
                state_v[c] + amp_vv * left[c]
            )
        gs = cot[:, 0:width]
        gv = [cot[:, (1 + c) * width : (2 + c) * width] for c in range(3)]
        grad_amp = jnp.concatenate(
            [gv[0] * left[0] + gv[1] * left[1] + gv[2] * left[2], gs * inner, gs], axis=1
        )
        grad_amp_low = grad_amp.astype(bf16)
        grad_w4 = mm(hidden, grad_amp_low, TN)
        for t in range(3):
            early_ref[(4 + t) * width : (5 + t) * width, :] += grad_w4[:, t * width : (t + 1) * width]
            bias_ref[1 + t : 2 + t, :] += jnp.sum(
                grad_amp[:, t * width : (t + 1) * width], axis=0, keepdims=True
            )
        slope = gate * (1.0 + pre * (1.0 - gate))
        grad_pre = mm(grad_amp_low, w4_ref[...], NT) * slope
        bias_ref[0:1, :] += jnp.sum(grad_pre, axis=0, keepdims=True)
        grad_pre_low = grad_pre.astype(bf16)
        early_ref[2 * width : 4 * width, :] += mm(joined, grad_pre_low, TN)
        grad_joined = mm(grad_pre_low, w3_ref[...], NT)
        mixed = gs * amp_sv
        ratio = grad_joined[:, width:] / norm
        grad_ref[pl.ds(first * TILE + 3, chunk, TILE), :] = gs + grad_joined[:, 0:width]
        grad_ref[pl.ds(first * TILE + 7, chunk, TILE), :] = jnp.ones((chunk, width), f32)
        grad_uv = None
        for c in range(3):
            grad_left = gv[c] * amp_vv + mixed * right[c]
            grad_right = mixed * left[c] + ratio * right[c]
            grad_both = jnp.concatenate([grad_left, grad_right], axis=1).astype(bf16)
            piece = mm(low[c], grad_both, TN)
            grad_uv = piece if grad_uv is None else grad_uv + piece
            grad_v = gv[c] + mm(grad_both, uv[...], NT)
            grad_ref[pl.ds(first * TILE + c, chunk, TILE), :] = grad_v
            grad_ref[pl.ds(first * TILE + 4 + c, chunk, TILE), :] = grad_v
        early_ref[0:width, :] += grad_uv[:, 0:width]
        early_ref[width : 2 * width, :] += grad_uv[:, width:]
        return carry

    lax.fori_loop(0, owned // chunk, update, 0)
    out_s_ref[...] = out_sc[:, 0:width].astype(bf16)
    out_v_ref[...] = out_sc[:, width:].astype(bf16)
    give_shares(place_y[0], early_ref, share_refs)


def places_of(sums, first, count):
    select = (iota((TILE, LANES), 0) == (iota((TILE, LANES), 1) & 7)).astype(bf16)
    value = sums[pl.ds(first * TILE + 7, count, TILE), :]
    high, middle, low = thirds(value)
    return (mm(select, high, NT) + mm(select, middle, NT)) + mm(select, low, NT)


def message_back(late_ref, weights, rows, part, own_grads):
    w1, b1, w2, b2 = weights
    width = LANES
    bias_at = 4 * width + 3 * ORDER_ROWS
    lead, pre, gate, hidden, filters = message_net(rows, w1, b1, w2, b2)
    vec = [rows[:, (1 + c) * width : (2 + c) * width] for c in range(3)]
    grad_filters = jnp.concatenate(
        [
            vec[0] * part[0] + vec[1] * part[1] + vec[2] * part[2],
            part[3],
            part[4] + part[5] + part[6],
        ],
        axis=1,
    )
    low = grad_filters.astype(bf16)
    grad_w2 = mm(hidden, low, TN)
    for t in range(3):
        late_ref[(1 + t) * width : (2 + t) * width, :] += grad_w2[:, t * width : (t + 1) * width]
        at = bias_at + 1 + t
        late_ref[at : at + 1, :] += jnp.sum(
            grad_filters[:, t * width : (t + 1) * width], axis=0, keepdims=True
        )
    grad_pre = mm(low, w2, NT) * (gate * (1.0 + pre * (1.0 - gate)))
    late_ref[bias_at : bias_at + 1, :] += jnp.sum(grad_pre, axis=0, keepdims=True)
    grad_pre_low = grad_pre.astype(bf16)
    late_ref[0:width, :] += mm(lead, grad_pre_low, TN)
    gate_vv = filters[:, 0:width]
    grads = [mm(grad_pre_low, w1, NT)] + [gate_vv * part[c] for c in range(3)]
    if own_grads is None:
        return grads
    return [x + y for x, y in zip(grads, own_grads)]


def backward_kernel(
    halo,
    shapes,
    listed,
    hub_listed,
    flat_table,
    flat_hub_table,
    targets,
    hub_list,
    hub_count,
    grads,
    bias_ref,
    tiles,
    basis_sc,
    slope_sc,
    geo_sc,
    w1_ref,
    b1_ref,
    w2_ref,
    b2_ref,
    wr_ref,
    br_ref,
    *rest,
):
    arrived, rest = arrived_views([h[1] for h in halo[::2]], shapes, rest)
    sums, target_sc, late_ref = rest[:3]
    rest = rest[3:]
    packets = rest[4 : 4 + shapes[2]]
    side_refs = list(rest[:4]) + pair_views(packets, packed_rows(halo[4][1]))
    rest = rest[4 + shapes[2] :]
    (
        filt,
        wext32,
        wext,
        turned_sc,
        coeff_sc,
        mix_sc,
        reduce_sc,
        spread_sc,
        radial_sc,
    ) = rest
    owned = grads.shape[0] // TILE
    width = LANES
    orders = wr_ref.shape[0]
    blocks = -(-owned // LANES)
    build_radial(wext32, wext, wr_ref, br_ref)
    hub_live = hub_count[0]
    rows = geo_sc.shape[0] // 6
    weights = (w1_ref[...], b1_ref[...], w2_ref[...], b2_ref[...])
    sums[...] = jnp.zeros(sums.shape, f32)
    radial_sc[...] = jnp.zeros(radial_sc.shape, f32)
    spread_sc[...] = jnp.zeros(spread_sc.shape, f32)
    reduce_sc[...] = jnp.zeros(reduce_sc.shape, f32)
    late_ref[...] = jnp.zeros(late_ref.shape, f32)

    def block_grads(b, count, trips, source_of, target_of):
        def mixes(pair, inner):
            for part in range(PARTS):
                i = pair * PARTS + part
                for n in range(TILE):
                    grad = source_at(grads, target_of(i, n))
                    for k in range(count):
                        filt[i, edge_at(k, n), :] = grad * source_at(tiles, source_of(i, k, n))
            return inner

        lax.fori_loop(0, trips, mixes, 0)
        span = min(listed, up_to(count, 4)) if count != listed else listed
        size = unrolled(span, 5)
        step = size * LANES

        def analyse(i, carry):
            first = i * step
            loaded = []
            for n in range(size):
                k = i * size + n
                part = [get_slot(filt, k, slot) for slot in range(7)]
                at = pl.ds(k * LANES, LANES)
                mix = [part[0] + part[1] + part[2], part[3], part[4], part[5], part[6]]
                for q in range(5):
                    mix_sc[at, q * width : (q + 1) * width] = mix[q].astype(bf16)
                row = b * SLOTS + k
                basis, scale = edge_coefficients(b, k, rows, basis_sc, geo_sc)
                loaded.append((basis, scale, order_tiles(slope_sc, row, rows)))
                plain, parts = scaled_parts(basis, scale)
                coeff = jnp.concatenate(plain + parts, axis=0)
                coeff_sc[:, at] = coeff.astype(bf16)
                turned_sc[at, :] = coeff.T.astype(bf16)
            mixes = mix_sc[pl.ds(first, step), :]
            backs = mm(wext[...], mixes, NT)
            radial_sc[...] += mm(coeff_sc[:, pl.ds(first, step)], mixes)
            for n, (basis, scale, slopes) in enumerate(loaded):
                back = backs[:, n * LANES : (n + 1) * LANES]
                total = None
                for t in range(ORDER_ROWS // TILE):
                    pieces = [
                        back[j * ORDER_ROWS + t * TILE : j * ORDER_ROWS + (t + 1) * TILE, :]
                        for j in range(4)
                    ]
                    mixed = (
                        pieces[0]
                        + pieces[1] * scale[1]
                        + pieces[2] * scale[2]
                        + pieces[3] * scale[3]
                    )
                    values = [mixed * basis[t], mixed * slopes[t]] + [
                        pieces[1 + c] * basis[t] for c in range(3)
                    ]
                    total = values if total is None else [x + y for x, y in zip(total, values)]
                for q in range(5):
                    at = q * TILE * SLOTS + i * size + n
                    reduce_sc[pl.ds(at, TILE, SLOTS), :] = total[q]
            return carry

        for i in range(span // size):
            analyse(i, 0)

        def geo(q):
            return geo_sc[pl.ds(pl.multiple_of(q * rows + b * SLOTS, SLOTS), SLOTS), :]

        factor = geo(0)
        direction = [geo(1 + c) for c in range(3)]
        slope = geo(4)
        inverse = geo(5)
        red = []
        for q in range(5):
            at = q * TILE * SLOTS
            pieces = [reduce_sc[at + n * SLOTS : at + (n + 1) * SLOTS] for n in range(TILE)]
            red.append(sum(pieces[1:], pieces[0]))
        grad_d = factor * red[1] + slope * red[0]
        grad_u = [factor * red[2 + c] for c in range(3)]
        along = (
            direction[0] * grad_u[0] + direction[1] * grad_u[1] + direction[2] * grad_u[2]
        )
        row = iota((SLOTS, LANES), 0)
        for c in range(3):
            value = (grad_u[c] - direction[c] * along) * inverse + grad_d * direction[c]
            value = jnp.where(row < count, value, 0.0)
            spread_sc[pl.ds(c, SLOTS, TILE), :] = value
            target_sc[b, c : c + 1, :] = -jnp.sum(value, axis=0, keepdims=True)
        turned = spread_sc[...].T
        group_of = iota((LANES, LANES), 1) >> 3
        fill_filters(
            span, turned_sc, wext, filt, width, lambda k: jnp.where(group_of == k, turned, 0.0)
        )

        def scatter(pair, inner):
            for part in range(PARTS):
                i = pair * PARTS + part
                for n in range(TILE):
                    grad = source_at(grads, target_of(i, n))
                    places = [
                        pl.ds(pl.multiple_of(source_of(i, k, n), TILE), TILE)
                        for k in range(count)
                    ]
                    held = [sums[at, :] for at in places]
                    fresh = [held[k] + grad * filt[i, edge_at(k, n), :] for k in range(count)]
                    for k in range(count):
                        sums[places[k], :] = fresh[k]
            return inner

        lax.fori_loop(0, trips, scatter, 0)

    target_sc[...] = jnp.zeros(target_sc.shape, f32)

    def regular_block(b, carry):
        base = b * LANES
        block_grads(
            b,
            listed,
            (jnp.minimum(LANES, owned - base) + PARTS * TILE - 1) // (PARTS * TILE),
            lambda i, k, n: flat_table[(base + i * TILE) * SLOTS + k * TILE + n],
            lambda i, n: targets[base + i * TILE + n],
        )
        return carry

    lax.fori_loop(0, blocks, regular_block, 0)
    block_grads(
        blocks,
        hub_listed,
        (hub_live + PARTS * TILE - 1) // (PARTS * TILE),
        lambda i, k, n: flat_hub_table[i * LANES + k * TILE + n],
        lambda i, n: hub_list[i * TILE + n] * TILE,
    )

    bias_at = 4 * width + 3 * ORDER_ROWS
    side_parts = []
    for first, count, _, _ in halo:
        count8 = up_to(count, TILE)
        part = [sums[pl.ds(first * TILE + slot, count8, TILE), :] for slot in range(7)]
        if count8 != count:
            keep = iota((count8, 1), 0) < count
            part = [jnp.where(keep, x, 0.0) for x in part]
        side_parts.append(part)
    side_rows = jnp.concatenate(
        [ref[0 : up_to(h[1], TILE), :] for h, ref in zip(halo, arrived)], axis=0
    )
    side_grads = message_back(
        late_ref, weights, side_rows, [jnp.concatenate(x, axis=0) for x in zip(*side_parts)], None
    )
    at = 0
    for index, (first, count, _, _) in enumerate(halo):
        count8 = up_to(count, TILE)
        side_ref = side_refs[index]
        side_ref[...] = jnp.zeros(side_ref.shape, f32)
        for q in range(4):
            side_ref[0:count8, q * width : (q + 1) * width] = side_grads[q][at : at + count8, :]
        at += count8
        write_places(side_ref, count, places_of(sums, first, count))

    for t in range(3):
        if t < 2:
            value = radial_sc[0:orders, t * width : (t + 1) * width]
            bias = radial_sc[orders : orders + 1, t * width : (t + 1) * width]
        else:
            value = None
            bias = None
            for c in range(3):
                at = (1 + c) * ORDER_ROWS
                lanes = slice((2 + c) * width, (3 + c) * width)
                one = radial_sc[at : at + orders, lanes]
                two = radial_sc[at + orders : at + orders + 1, lanes]
                value = one if value is None else value + one
                bias = two if bias is None else bias + two
        late_ref[4 * width + t * ORDER_ROWS : 4 * width + t * ORDER_ROWS + orders, :] = value
        late_ref[bias_at + 4 + t : bias_at + 5 + t, :] = bias

    late_ref[bias_at + 7 : bias_at + 11, :] = bias_ref[0:4, :]


def own_back_kernel(
    shares,
    me,
    sums,
    target_ref,
    late_in,
    s_ref,
    v_ref,
    grads,
    names_ref,
    hub_row_ref,
    w1_ref,
    b1_ref,
    w2_ref,
    b2_ref,
    *rest,
):
    early, rest = rest[:shares], rest[shares:]
    own_ref, place_ref, early_ref = rest[:3]
    share_refs, late_ref = rest[3:-1], rest[-1]
    early_ref[...] = summed(early)
    owned = s_ref.shape[0]
    rows = jnp.concatenate([s_ref[...].astype(f32), v_ref[...].astype(f32)], axis=1)
    width = LANES
    hubs = hub_row_ref.shape[1]
    blocks = -(-owned // LANES)
    weights = (w1_ref[...], b1_ref[...], w2_ref[...], b2_ref[...])
    late_ref[...] = late_in[...]
    parts = [sums[pl.ds(slot, owned, TILE), :] for slot in range(7)]
    held = [grads[pl.ds(slot, owned, TILE), :] for slot in (3, 0, 1, 2)]
    own_grads = message_back(late_ref, weights, rows, parts, held)
    for q in range(4):
        own_ref[:, q * width : (q + 1) * width] = own_grads[q]
    give_shares(me[0], late_ref, share_refs)
    place_ref[...] = places_of(sums, 0, owned)
    total = None
    for b in range(blocks + 1):
        names = hub_row_ref[...] * TILE if b == blocks else names_ref[b : b + 1, :]
        onehot = (iota((owned, hubs), 0) * TILE == jnp.broadcast_to(names, (owned, hubs))).astype(bf16)
        part = pick_exact(target_ref[b], onehot)
        total = part if total is None else total + part
    place_ref[...] += total


def chunk_of(ref, me, shift, count):
    size = ref.shape[0] // count
    at = lax.rem(me + shift, count) * size
    return ref[pl.ds(pl.multiple_of(at, TILE), size), :]


def give_shares(me, ref, share_refs):
    for t, share_ref in enumerate(share_refs):
        share_ref[...] = chunk_of(ref, me, t, len(share_refs))


def gathered_back(first, count, pieces):
    rows = sum(list_ref.shape[1] for _, list_ref, _ in pieces)
    target = iota((count, rows), 0) + first
    names = jnp.concatenate(
        [
            jnp.broadcast_to(list_ref[side : side + 1, :], (TILE, list_ref.shape[1]))
            for _, list_ref, side in pieces
        ],
        axis=1,
    )
    onehot = (target == names[0:1, :]).astype(bf16)
    values = jnp.concatenate(
        [ref[0 : list_ref.shape[1], :] for ref, list_ref, _ in pieces], axis=0
    ).astype(bf16)
    places = jnp.concatenate(
        [read_places(ref, list_ref.shape[1])[:, 0 : list_ref.shape[1]] for ref, list_ref, _ in pieces],
        axis=1,
    )
    return mm(onehot, values), pick_exact(places, onehot)


def list_pieces(lists, arrived):
    pieces = []
    for n, list_ref in enumerate(lists):
        pieces += [(arrived[2 * n], list_ref, 0), (arrived[2 * n + 1], list_ref, 1)]
    return pieces


def add_back(first, count, pieces, part_ref, out_ref):
    count8 = up_to(count, TILE)
    total, places = gathered_back(first, count8, pieces)
    if count8 != count:
        total = jnp.where(iota((count8, 1), 0) < count, total, 0.0)
    rows = part_ref.shape[0]
    out_ref[0:rows, :] = part_ref[...]
    out_ref[0:count8, :] += total
    write_places(out_ref, count, read_places(part_ref, count)[:, 0:count] + places[:, 0:count])


def return_y_kernel(ranges, sizes, me, z_list, *refs):
    size_z, size_y = sizes
    z_size = 1 if size_z == 2 else 2
    y_size = 1 if size_y == 2 else 2
    packets, refs = refs[:z_size], refs[z_size:]
    late, refs = refs[:size_y], refs[size_y:]
    early, refs = refs[0], refs[1:]
    partial, refs = refs[:2], refs[2:]
    outs, refs = refs[:y_size], refs[y_size:]
    share_refs, share = refs[:-1], refs[-1]
    size = late[0].shape[0]
    share[0:size, :] = summed(late)
    share[size:, :] = early[...]
    give_shares(me[0], share, share_refs)
    arrived, _ = arrived_views([z_list.shape[1]], [z_size], packets)
    pieces = list_pieces([z_list], arrived)
    y_rows = packed_rows(ranges[0][1])
    for (first, count), part_ref, out_ref in zip(ranges, partial, pair_views(outs, y_rows)):
        add_back(first, count, pieces, part_ref, out_ref)


def return_x_kernel(ranges, sizes, z_list, y_list, *refs):
    size_z, size_y = sizes
    shapes = [1 if size == 2 else 2 for size in sizes]
    arrived, rest = arrived_views([z_list.shape[1], y_list.shape[1]], shapes, refs)
    shares, rest = rest[:size_z], rest[size_z:]
    partial, rest = rest[:2], rest[2:]
    outs, keep_x = rest[:-1], rest[-1]
    keep_x[...] = summed(shares)
    x_rows = packed_rows(ranges[0][1])
    pieces = list_pieces([z_list, y_list], arrived)
    for (first, count), part_ref, out_ref in zip(ranges, partial, pair_views(outs, x_rows)):
        add_back(first, count, pieces, part_ref, out_ref)


def own_kernel(shapes, *refs):
    phases = len(shapes)
    lists = refs[:phases]
    arrived, rest = arrived_views([x.shape[1] for x in lists], shapes, refs[phases:])
    own_ref, place_ref, *outs = rest
    total, places = gathered_back(0, own_ref.shape[0], list_pieces(lists, arrived))
    total = total + own_ref[...]
    places = places + place_ref[...]
    if len(outs) == 2:
        outs[0][...] = total
        outs[1][...] = places
    else:
        outs[0][...] = total[:, 0:LANES]
        outs[1][...] = total[:, LANES:]
        outs[2][...] = places[0:3, :]


def summed(refs):
    total = refs[0][...]
    for ref in refs[1:]:
        total = total + ref[...]
    return total


def sum_kernel(*refs):
    refs[-1][...] = summed(refs[:-1])


def join_kernel(me, *refs):
    shares, out_ref = refs[:-1], refs[-1]
    count = len(shares)
    size = shares[0].shape[0]
    for t in range(count):
        at = lax.rem(me[0] + count - t, count) * size
        out_ref[pl.ds(pl.multiple_of(at, TILE), size), :] = shares[t][...]


def gather_order(me, count):
    if count != 4:
        return [lax.rem(me + count - t, count) for t in range(count)]
    beside = me + 1 - 2 * lax.rem(me, 2)
    return [me, beside, lax.rem(me + 2, 4), lax.rem(beside + 2, 4)]


def unpack_kernel(sizes, late_share, me, *refs):
    size_y, size_z = sizes
    late_ref, early_ref, joined = refs[-3:]
    outs = refs[size_y:-3]
    share = late_share + early_ref.shape[0] // size_y
    for t, owner in enumerate(gather_order(me[0], size_y)):
        joined[pl.ds(pl.multiple_of(owner * share, TILE), share), :] = refs[t][...]
    rest = share - late_share
    for n in range(size_y):
        late_ref[n * late_share : (n + 1) * late_share, :] = joined[
            n * share : n * share + late_share, :
        ]
        early_ref[n * rest : (n + 1) * rest, :] = joined[n * share + late_share : (n + 1) * share, :]
    (w1, b1, w2, b2, wr, br, u, v, w3, b3, w4, b4) = outs
    width = LANES
    orders = wr.shape[0]
    bias_at = 4 * width + 3 * ORDER_ROWS
    u[...] = early_ref[0:width, :]
    v[...] = early_ref[width : 2 * width, :]
    w3[...] = early_ref[2 * width : 4 * width, :]
    b3[...] = late_ref[bias_at + 7, :]
    w1[...] = late_ref[0:width, :]
    b1[...] = late_ref[bias_at, :]
    for t in range(3):
        lanes = slice(t * width, (t + 1) * width)
        w4[:, lanes] = early_ref[(4 + t) * width : (5 + t) * width, :]
        b4[lanes] = late_ref[bias_at + 8 + t, :]
        w2[:, lanes] = late_ref[(1 + t) * width : (2 + t) * width, :]
        b2[lanes] = late_ref[bias_at + 1 + t, :]
        at = 4 * width + t * ORDER_ROWS
        wr[:, lanes] = late_ref[at : at + orders, :]
        br[lanes] = late_ref[bias_at + 4 + t, :]


def work(array, operations):
    return pl.CostEstimate(
        flops=operations, bytes_accessed=4 * array.size * array.dtype.itemsize, transcendentals=0
    )


def exchange(axis, packets):
    count = lax.axis_size(axis)
    up = [(i, (i + 1) % count) for i in range(count)]
    if len(packets) == 1:
        return [lax.ppermute(packets[0], axis, up)]
    down = [(j, i) for i, j in up]
    return [lax.ppermute(packets[1], axis, up), lax.ppermute(packets[0], axis, down)]


def rotated(axis, pieces):
    count = lax.axis_size(axis)
    return [pieces[0]] + [
        lax.ppermute(pieces[t], axis, [(i, (i + t) % count) for i in range(count)])
        for t in range(1, count)
    ]


def gathered(axis, piece):
    if lax.axis_size(axis) != 4:
        return rotated(axis, [piece] * lax.axis_size(axis))
    beside = [(i, i ^ 1) for i in range(4)]
    across = lax.ppermute(piece, axis, [(i, (i + 2) % 4) for i in range(4)])
    near = lax.ppermute(piece, axis, beside)
    return [piece, near, across, lax.ppermute(across, axis, beside)]


def local(
    scalar_feat,
    vector_feat,
    positions,
    message_inner,
    message_inner_bias,
    message_outer,
    message_outer_bias,
    radial_weight,
    radial_bias,
    update_left,
    update_right,
    update_inner,
    update_inner_bias,
    update_outer,
    update_outer_bias,
    scalar_cotangent,
    vector_cotangent,
    x_face_rows,
    y_face_rows,
    z_face_rows,
    neighbour_table,
    hub_atoms,
    hub_table,
    hub_count,
):
    owned, width = scalar_feat.shape
    length = G * SPACING
    counts = [x_face_rows.shape[2], y_face_rows.shape[2], z_face_rows.shape[2]]
    lists = [x_face_rows[0], y_face_rows[0], z_face_rows[0]]
    axes = ("gx", "gy", "gz")
    halo = []
    first = owned
    for number, count in enumerate(counts):
        halo.append((first, count, number, -length))
        halo.append((first + count, count, number, length))
        first += 2 * count
    ext = first
    packets, (rows, place, y_list, z_list) = first_pack(
        axes[0], lists, scalar_feat, vector_feat, positions
    )
    lists = [lists[0], y_list, z_list]
    arrived = exchange(axes[0], packets)
    shapes = [len(packets)]
    own_packs = pack_own(lists[1:], rows, place)
    table, flat_table, flat_hub_table, names, target_place = order_atoms(
        neighbour_table, hub_table, place
    )
    for number in range(1, 3):
        own = own_packs[2 * number - 2 : 2 * number]
        packets = pack_sides(
            axes[number], lists[number], own, halo[: 2 * number], shapes, arrived
        )
        packets, names = lax.optimization_barrier((packets, names))
        arrived = arrived + exchange(axes[number], packets)
        shapes.append(len(packets))
    shapes = tuple(shapes)

    cots = jnp.concatenate([scalar_cotangent, vector_cotangent], axis=1).astype(f32)
    flat_table = flat_table.reshape(-1)
    flat_hub_table = flat_hub_table.reshape(-1)
    targets = names.reshape(-1)
    hub_row = hub_atoms.reshape(1, -1)
    b1 = message_inner_bias.reshape(1, -1)
    b2 = message_outer_bias.reshape(1, -1)
    br = radial_bias.reshape(1, -1)
    b3 = update_inner_bias.reshape(1, -1)
    b4 = update_outer_bias.reshape(1, -1)

    blocks = -(-owned // LANES)
    chunk = owned
    ext_tiles = up_to(ext, TILE) * TILE
    slots = neighbour_table.shape[0]
    assert slots <= SLOTS and hub_table.shape[0] <= slots and owned % TILE == 0
    assert hub_atoms.shape[0] == LANES and blocks <= TILE
    hub_slots = hub_table.shape[0]
    inner_rows = up_to(blocks, GROUP) * SLOTS
    smem = pl.BlockSpec(memory_space=pltpu.SMEM)
    vmem = pl.BlockSpec(memory_space=pltpu.VMEM)
    small = pltpu.CompilerParams(vmem_limit_bytes=8 * MIB)
    middle = pltpu.CompilerParams(vmem_limit_bytes=20 * MIB)
    wide = 5 * width
    size_x, size_y, size_z = [lax.axis_size(axis) for axis in axes]
    step = TILE * size_y * size_z
    late_rows = up_to(4 * width + 3 * ORDER_ROWS + 2 * TILE, step)
    early_rows = up_to(7 * width, step)
    late_share = jax.ShapeDtypeStruct((late_rows // size_y, width), f32)
    early_share = jax.ShapeDtypeStruct((early_rows // size_y, width), f32)
    share_y = jax.ShapeDtypeStruct(((late_rows + early_rows) // size_y, width), f32)
    share_z = jax.ShapeDtypeStruct((share_y.shape[0] // size_z, width), f32)
    me_y = lax.axis_index("gy").reshape(1)
    me_z = lax.axis_index("gz").reshape(1)
    geo_rows = up_to(blocks + 1, GROUP) * SLOTS
    shared = [
        pltpu.VMEM((TILE, up_to(ext, LANES)), f32),
        pltpu.VMEM((geo_rows, LANES), jnp.int32),
        pltpu.VMEM((3 * geo_rows, LANES), f32),
    ]
    inner_sums = pl.pallas_call(
        functools.partial(inner_kernel, slots),
        in_specs=[smem] * 2 + [vmem] * 10,
        out_shape=jax.ShapeDtypeStruct((owned * TILE, LANES), f32),
        scratch_shapes=[
            pltpu.VMEM((owned * TILE, LANES), f32),
            pltpu.VMEM((LANES // TILE, slots * TILE * STEP, LANES), f32),
            pltpu.VMEM((TILE, blocks * LANES), f32),
            pltpu.VMEM((inner_rows, LANES), jnp.int32),
            pltpu.VMEM((3 * inner_rows, LANES), f32),
            pltpu.VMEM((ORDER_ROWS * inner_rows, LANES), f32),
            pltpu.VMEM((6 * inner_rows, LANES), f32),
            pltpu.VMEM((4 * ORDER_ROWS, wide), f32),
            pltpu.VMEM((4 * ORDER_ROWS, wide), bf16),
        ],
        compiler_params=pltpu.CompilerParams(vmem_limit_bytes=24 * MIB),
        cost_estimate=work(rows, 2 * geo_rows * LANES * 4 * ORDER_ROWS * wide * 3),
        name="edges_inner",
    )(
        flat_table,
        targets,
        rows,
        place,
        table,
        target_place,
        message_inner,
        b1,
        message_outer,
        b2,
        radial_weight,
        br,
    )
    out_s, out_v, grad, bias, *tables = pl.pallas_call(
        functools.partial(
            forward_kernel, tuple(halo), shapes, slots, hub_slots, chunk, size_y
        ),
        in_specs=[smem] * 6 + [vmem] * (20 + len(arrived)),
        out_shape=(
            jax.ShapeDtypeStruct((owned, width), bf16),
            jax.ShapeDtypeStruct((owned, 3 * width), bf16),
            jax.ShapeDtypeStruct((owned * TILE, width), f32),
            jax.ShapeDtypeStruct((TILE, width), f32),
            jax.ShapeDtypeStruct((ext_tiles, LANES), f32),
            jax.ShapeDtypeStruct((ORDER_ROWS * geo_rows, LANES), f32),
            jax.ShapeDtypeStruct((ORDER_ROWS * geo_rows, LANES), f32),
            jax.ShapeDtypeStruct((6 * geo_rows, LANES), f32),
        )
        + (early_share,) * size_y,
        scratch_shapes=[
            pltpu.VMEM((LANES // TILE, slots * TILE * STEP, LANES), f32),
            pltpu.VMEM((owned * TILE, LANES), f32),
        ]
        + shared
        + [
            pltpu.VMEM((4 * ORDER_ROWS, wide), f32),
            pltpu.VMEM((4 * ORDER_ROWS, wide), bf16),
            pltpu.VMEM((width, 2 * width), bf16),
            pltpu.VMEM((owned, 4 * width), f32),
            pltpu.VMEM((early_rows, width), f32),
        ],
        compiler_params=pltpu.CompilerParams(vmem_limit_bytes=24 * MIB),
        name="edges_forward",
    )(
        flat_table,
        flat_hub_table,
        targets,
        hub_atoms,
        hub_count,
        me_y,
        rows,
        place,
        cots,
        table,
        target_place,
        hub_table,
        hub_row,
        inner_sums,
        message_inner,
        b1,
        message_outer,
        b2,
        radial_weight,
        br,
        update_left,
        update_right,
        update_inner,
        b3,
        update_outer,
        b4,
        *arrived,
    )
    tables, early = tables[:4], rotated("gy", tables[4:])
    results = pl.pallas_call(
        functools.partial(backward_kernel, tuple(halo), shapes, slots, hub_slots),
        in_specs=[smem] * 5 + [vmem] * (12 + len(arrived)),
        out_shape=(
            jax.ShapeDtypeStruct((ext_tiles, LANES), f32),
            jax.ShapeDtypeStruct((blocks + 1, TILE, LANES), f32),
            jax.ShapeDtypeStruct((late_rows, width), f32),
        )
        + tuple(
            jax.ShapeDtypeStruct((packed_rows(count), 4 * width), f32)
            for count in (counts[0], counts[0], counts[1], counts[1])
        )
        + tuple(packet_shapes("gz", counts[2], 4 * width, 0)),
        scratch_shapes=[
            pltpu.VMEM((LANES // TILE, slots * TILE * STEP, LANES), f32),
            pltpu.VMEM((4 * ORDER_ROWS, wide), f32),
            pltpu.VMEM((4 * ORDER_ROWS, wide), bf16),
            pltpu.VMEM((slots * LANES, 4 * ORDER_ROWS), bf16),
            pltpu.VMEM((4 * ORDER_ROWS, slots * LANES), bf16),
            pltpu.VMEM((slots * LANES, wide), bf16),
            pltpu.VMEM((5 * TILE * SLOTS, LANES), f32),
            pltpu.VMEM((LANES, LANES), f32),
            pltpu.VMEM((4 * ORDER_ROWS, wide), f32),
        ],
        compiler_params=pltpu.CompilerParams(vmem_limit_bytes=22 * MIB),
        cost_estimate=work(rows, 2 * geo_rows * LANES * 4 * ORDER_ROWS * wide * 12),
        name="edges_backward",
    )(
        flat_table,
        flat_hub_table,
        targets,
        hub_atoms,
        hub_count,
        grad,
        bias,
        *tables,
        message_inner,
        b1,
        message_outer,
        b2,
        radial_weight,
        br,
        *arrived,
    )
    sums, target, late = results[:3]
    sides = results[3:7]
    packets, early = lax.optimization_barrier((results[7:], early))
    back_z = exchange("gz", packets)
    own, place, early, *late = pl.pallas_call(
        functools.partial(own_back_kernel, size_y),
        in_specs=[smem] + [vmem] * (12 + size_y),
        out_shape=(
            jax.ShapeDtypeStruct((owned, 4 * width), f32),
            jax.ShapeDtypeStruct((TILE, owned), f32),
            early_share,
        )
        + (late_share,) * size_y,
        scratch_shapes=[pltpu.VMEM((late_rows, width), f32)],
        compiler_params=pltpu.CompilerParams(vmem_limit_bytes=14 * MIB),
        name="own_backward",
    )(me_y, sums, target, late, scalar_feat, vector_feat, grad, names, hub_row, message_inner, b1, message_outer, b2, *early)
    ranges = [(h[0], h[1]) for h in halo]

    late = rotated("gy", late)
    results = pl.pallas_call(
        functools.partial(return_y_kernel, tuple(ranges[2:4]), (size_z, size_y)),
        in_specs=[smem] + [vmem] * (1 + shapes[2] + size_y + 3),
        out_shape=tuple(packet_shapes("gy", counts[1], 4 * width, 0)) + (share_z,) * size_z,
        scratch_shapes=[pltpu.VMEM(share_y.shape, f32)],
        compiler_params=middle,
        name="return_y",
    )(me_z, lists[2], *back_z, *late, early, *sides[2:4])
    packets, shares = results[: shapes[1]], results[shapes[1] :]

    shares = rotated("gz", shares)
    back_y = exchange("gy", packets)
    results = pl.pallas_call(
        functools.partial(return_x_kernel, tuple(ranges[0:2]), (size_z, size_y)),
        out_shape=tuple(packet_shapes("gx", counts[0], 4 * width, 0)) + (share_z,),
        compiler_params=middle,
        name="return_x",
    )(lists[2], lists[1], *back_z, *back_y, *shares, *sides[0:2])
    packets, keep = results[:-1], results[-1]

    shares = rotated("gx", [keep] * size_x)
    total = pl.pallas_call(
        sum_kernel, out_shape=share_z, compiler_params=small, name="sum_last"
    )(*shares)
    packets, total = lax.optimization_barrier((packets, total))
    shares = rotated("gz", [total] * size_z)
    back_x = exchange("gx", packets)
    own, place = pl.pallas_call(
        functools.partial(own_kernel, (shapes[2], shapes[1])),
        out_shape=(
            jax.ShapeDtypeStruct(own.shape, f32),
            jax.ShapeDtypeStruct(place.shape, f32),
        ),
        compiler_params=middle,
        cost_estimate=work(own, 2 * owned * 4 * width * 1056),
        name="own_partial",
    )(lists[2], lists[1], *back_z, *back_y, own, place)
    total = pl.pallas_call(
        join_kernel,
        in_specs=[smem] + [vmem] * size_z,
        out_shape=share_y,
        compiler_params=small,
        name="join_shares",
    )(me_z, *shares)
    total, own, place = lax.optimization_barrier((total, own, place))
    shares = gathered("gy", total)
    scalar_grad, vector_grad, positions_grad = pl.pallas_call(
        functools.partial(own_kernel, (shapes[0],)),
        out_shape=(
            jax.ShapeDtypeStruct((owned, width), f32),
            jax.ShapeDtypeStruct((owned, 3 * width), f32),
            jax.ShapeDtypeStruct((3, owned), f32),
        ),
        compiler_params=middle,
        cost_estimate=work(own, 2 * owned * 4 * width * 400),
        name="own_last",
    )(lists[0], *back_x, own, place)

    def like(x):
        return jax.ShapeDtypeStruct(x.shape, f32)

    weights = pl.pallas_call(
        functools.partial(unpack_kernel, (size_y, size_z), late_share.shape[0]),
        in_specs=[smem] + [vmem] * size_y,
        out_shape=tuple(
            like(x)
            for x in (
                message_inner,
                message_inner_bias,
                message_outer,
                message_outer_bias,
                radial_weight,
                radial_bias,
                update_left,
                update_right,
                update_inner,
                update_inner_bias,
                update_outer,
                update_outer_bias,
            )
        ),
        scratch_shapes=[
            pltpu.VMEM((late_rows, width), f32),
            pltpu.VMEM((early_rows, width), f32),
            pltpu.VMEM((late_rows + early_rows, width), f32),
        ],
        compiler_params=small,
        name="unpack_weights",
    )(me_y, *shares)
    return (out_s, out_v, scalar_grad, vector_grad, positions_grad, *weights)


def solution(mesh):
    cells = P(("gx", "gy", "gz"), None)
    columns = P(None, ("gx", "gy", "gz"))
    faces = P(("gx", "gy", "gz"), None, None)
    flat = P(("gx", "gy", "gz"))
    return jax.shard_map(
        local,
        mesh=mesh,
        in_specs=(cells, cells, columns)
        + (P(),) * 12
        + (cells, cells, faces, faces, faces, columns, flat, columns, flat),
        out_specs=(cells, cells, cells, cells, columns) + (P(),) * 12,
        check_vma=False,
    )
```

```python
import functools
import math

import jax
import jax.numpy as jnp
from jax import lax
from jax.experimental import pallas as pl
from jax.experimental.pallas import tpu as pltpu
from jax.sharding import PartitionSpec as P

G = 10
SPACING = 2.6
CUTOFF = 5.0

LANES = 128
TILE = 8
STEP = 9
SLOTS = 16
ORDER_ROWS = 24
GROUP = 3
MIB = 1024 * 1024
f32 = jnp.float32
bf16 = jnp.bfloat16

NN = ((1,), (0,))
NT = ((1,), (1,))
TN = ((0,), (0,))


def up_to(count, step):
    return -(-count // step) * step


def mm(left_side, right_side, dims=NN):
    return lax.dot_general(
        left_side, right_side, (dims, ((), ())), preferred_element_type=f32
    )


def halves(x):
    high = x.astype(bf16)
    return high, (x - high.astype(f32)).astype(bf16)


def thirds(x):
    high = x.astype(bf16)
    rest = x - high.astype(f32)
    middle = rest.astype(bf16)
    return high, middle, (rest - middle.astype(f32)).astype(bf16)


def pick_exact(values, onehot):
    stacked = jnp.concatenate([x.astype(f32) for x in thirds(values)], axis=0).astype(bf16)
    moved = mm(stacked, onehot, NT)
    return (moved[0:TILE] + moved[TILE : 2 * TILE]) + moved[2 * TILE :]


def packed_rows(count):
    return up_to(count + -(-count // LANES), TILE)


def iota(shape, dim):
    return lax.broadcasted_iota(jnp.int32, shape, dim)


def read_places(ref, count):
    pieces = []
    sub = iota((TILE, LANES), 0)
    for part in range(-(-count // LANES)):
        row = count + part
        rows = [
            jnp.broadcast_to(ref[row : row + 1, c * LANES : (c + 1) * LANES], (TILE, LANES))
            for c in range(3)
        ]
        pieces.append(
            jnp.where(sub == 0, rows[0], jnp.where(sub == 1, rows[1], jnp.where(sub == 2, rows[2], 0.0)))
        )
    return pieces[0] if len(pieces) == 1 else jnp.concatenate(pieces, axis=1)


def write_places(ref, count, places):
    width = places.shape[1]
    for part in range(-(-count // LANES)):
        size = min(LANES, width - part * LANES)
        for c in range(3):
            ref[count + part : count + part + 1, c * LANES : c * LANES + size] = places[
                c : c + 1, part * LANES : part * LANES + size
            ]


def shifted_places(ref, count, axis_number, amount):
    places = read_places(ref, count)
    sub = iota(places.shape, 0)
    return places + jnp.where(sub == axis_number, amount, 0.0)


def pair_views(refs, rows):
    if len(refs) == 2:
        return list(refs)
    return [refs[0].at[pl.ds(0, rows)], refs[0].at[pl.ds(rows, rows)]]


def arrived_views(counts, shapes, refs):
    views = []
    at = 0
    for count, size in zip(counts, shapes):
        pair = pair_views(refs[at : at + size], packed_rows(count))
        views += pair if size == 2 else pair[::-1]
        at += size
    return views, refs[at:]


def pack_rows(halo, arrived, list_sc, rows, place, count, out_refs):
    owned = rows.shape[0]
    count8 = up_to(count, TILE)
    columns = list_sc[...].T
    for side, out_ref in enumerate(out_refs):
        column = columns[0:count8, side : side + 1]
        out_ref[...] = jnp.zeros(out_ref.shape, f32)
        onehot = (column == iota((count8, owned), 1).astype(f32)).astype(bf16)
        total = mm(onehot, rows)
        places = pick_exact(place, onehot)
        for (first, size, axis_number, amount), ref in zip(halo, arrived):
            size8 = up_to(size, TILE)
            lane = iota((count8, size8), 1)
            onehot = ((column == (lane + first).astype(f32)) & (lane < size)).astype(bf16)
            total = total + mm(onehot, ref[0:size8, :].astype(bf16))
            arrived_places = shifted_places(ref, size, axis_number, amount)
            places = places + pick_exact(arrived_places[:, 0:size8], onehot)
        out_ref[0:count8, :] = total
        write_places(out_ref, count, places)


def first_pack_kernel(out_size, x_hbm, y_hbm, z_hbm, s_hbm, v_hbm, p_hbm, *rest):
    outs = rest[:out_size]
    (
        rows_ref,
        place_ref,
        y_out,
        z_out,
        x_ref,
        s_ref,
        v_ref,
        p_ref,
        list_sc,
        sems,
    ) = rest[out_size:]
    pairs = (
        (x_hbm, x_ref),
        (s_hbm, s_ref),
        (v_hbm, v_ref),
        (p_hbm, p_ref),
        (y_hbm, y_out),
        (z_hbm, z_out),
    )
    copies = [pltpu.make_async_copy(a, b, sems.at[n]) for n, (a, b) in enumerate(pairs)]
    for copy in copies:
        copy.start()
    count = x_ref.shape[1]
    place_ref[...] = jnp.zeros(place_ref.shape, f32)
    list_sc[...] = jnp.full(list_sc.shape, -1.0, f32)
    for copy in copies:
        copy.wait()
    list_sc[0:2, 0:count] = x_ref[...].astype(f32)
    place_ref[0:3, :] = p_ref[...]
    rows = jnp.concatenate([s_ref[...], v_ref[...]], axis=1)
    out_refs = pair_views(outs, packed_rows(count))
    pack_rows((), (), list_sc, rows, place_ref[...], count, out_refs)
    rows_ref[...] = rows.astype(f32)


def list_to(list_sc, list_ref):
    list_sc[...] = jnp.full(list_sc.shape, -1.0, f32)
    list_sc[0:2, 0 : list_ref.shape[1]] = list_ref[...].astype(f32)


def pack_own_kernel(y_list, z_list, rows_ref, place_ref, *rest):
    outs, list_sc = rest[:4], rest[4]
    rows = rows_ref[...].astype(bf16)
    for n, list_ref in enumerate((y_list, z_list)):
        list_to(list_sc, list_ref)
        pair = outs[2 * n : 2 * n + 2]
        pack_rows((), (), list_sc, rows, place_ref[...], list_ref.shape[1], pair)


def pack_kernel(halo, shapes, out_size, list_ref, own_lower, own_upper, *rest):
    arrived, rest = arrived_views([h[1] for h in halo[::2]], shapes, rest)
    count = list_ref.shape[1]
    count8 = up_to(count, TILE)
    out_refs = pair_views(rest[:out_size], packed_rows(count))
    list_sc = rest[out_size]
    list_to(list_sc, list_ref)
    columns = list_sc[...].T
    sizes = [up_to(h[1], TILE) for h in halo]
    values = jnp.concatenate(
        [ref[0:size, :] for size, ref in zip(sizes, arrived)], axis=0
    ).astype(bf16)
    for side, (own_ref, out_ref) in enumerate(zip((own_lower, own_upper), out_refs)):
        column = columns[0:count8, side : side + 1]
        pieces = []
        places = read_places(own_ref, count)[:, 0:count8]
        for (first, size, axis_number, amount), size8, ref in zip(halo, sizes, arrived):
            lane = iota((count8, size8), 1)
            onehot = ((column == (lane + first).astype(f32)) & (lane < size)).astype(bf16)
            pieces.append(onehot)
            moved = shifted_places(ref, size, axis_number, amount)
            places = places + pick_exact(moved[:, 0:size8], onehot)
        out_ref[...] = own_ref[...]
        total = own_ref[0:count8, :]
        at = 0
        for size8, onehot in zip(sizes, pieces):
            total = total + mm(onehot, values[at : at + size8, :])
            at += size8
        out_ref[0:count8, :] = total
        write_places(out_ref, count, places)


def packet_shapes(axis, count, width, extra):
    rows = packed_rows(count)
    if lax.axis_size(axis) == 2:
        return [jax.ShapeDtypeStruct((2 * rows + extra, width), f32)]
    return [jax.ShapeDtypeStruct((rows + extra, width), f32)] * 2


def first_pack(axis, lists, s, v, p):
    owned, width = s.shape
    count = lists[0].shape[1]
    out = packet_shapes(axis, count, 4 * width, 0)
    far = pl.BlockSpec(memory_space=pltpu.HBM)
    inputs = [pltpu.with_memory_space_constraint(x, pltpu.HBM) for x in (*lists, s, v, p)]
    results = pl.pallas_call(
        functools.partial(first_pack_kernel, len(out)),
        in_specs=[far] * 6,
        out_shape=tuple(out)
        + (
            jax.ShapeDtypeStruct((owned, 4 * width), f32),
            jax.ShapeDtypeStruct((TILE, owned), f32),
        )
        + tuple(jax.ShapeDtypeStruct(x.shape, x.dtype) for x in lists[1:]),
        scratch_shapes=[
            pltpu.VMEM(lists[0].shape, lists[0].dtype),
            pltpu.VMEM(s.shape, s.dtype),
            pltpu.VMEM(v.shape, v.dtype),
            pltpu.VMEM(p.shape, p.dtype),
            pltpu.VMEM((TILE, up_to(count, LANES)), f32),
            pltpu.SemaphoreType.DMA((6,)),
        ],
        compiler_params=pltpu.CompilerParams(vmem_limit_bytes=14 * MIB),
        name="pack_first",
    )(*inputs)
    return list(results[: len(out)]), results[len(out) :]


def pack_own(lists, rows, place):
    shapes = []
    for list_ref in lists:
        shapes += [jax.ShapeDtypeStruct((packed_rows(list_ref.shape[1]), rows.shape[1]), f32)] * 2
    longest = max(list_ref.shape[1] for list_ref in lists)
    return pl.pallas_call(
        pack_own_kernel,
        out_shape=tuple(shapes),
        scratch_shapes=[pltpu.VMEM((TILE, up_to(longest, LANES)), f32)],
        compiler_params=pltpu.CompilerParams(vmem_limit_bytes=14 * MIB),
        name="pack_own",
    )(*lists, rows, place)


def pack_sides(axis, lists, own, halo, shapes, arrived):
    count = lists.shape[1]
    out = packet_shapes(axis, count, own[0].shape[1], 0)
    return pl.pallas_call(
        functools.partial(pack_kernel, tuple(halo), tuple(shapes), len(out)),
        out_shape=tuple(out),
        scratch_shapes=[pltpu.VMEM((TILE, up_to(count, LANES)), f32)],
        compiler_params=pltpu.CompilerParams(vmem_limit_bytes=14 * MIB),
        name="pack_rows",
    )(lists, *own, *arrived)


def build_places(place_sc, p_ref, owned, halo, arrived):
    place_sc[...] = jnp.zeros(place_sc.shape, f32)
    place_sc[:, 0:owned] = p_ref[...]
    for (first, rows, axis_number, amount), ref in zip(halo, arrived):
        places = shifted_places(ref, rows, axis_number, amount)
        place_sc[:, first : first + rows] = places[:, 0:rows]


def order_kernel(
    table_ref,
    hub_table_ref,
    place_ref,
    table_out,
    flat_out,
    hub_out,
    target_out,
    place_out,
    wide_sc,
    stack_sc,
    tall_sc,
):
    listed, owned = table_ref.shape
    slots = wide_sc.shape[1]
    wide_sc[...] = jnp.zeros(wide_sc.shape, jnp.int32)
    wide_sc[0:listed, 0:owned] = table_ref[...]
    lane = iota((1, slots), 1)
    worst = jnp.max(wide_sc[...].astype(f32), axis=0, keepdims=True)
    inner = (worst < owned) & (lane < owned)
    flag = inner.astype(f32)
    before = (iota((slots, slots), 0) <= iota((slots, slots), 1)).astype(bf16)
    count = mm(jnp.broadcast_to(flag, (TILE, slots)).astype(bf16), before)[0:1, :]
    total = count[:, slots - 1 : slots]
    index = lane.astype(f32)
    slot = jnp.where(inner, count - 1.0, total + index - count)
    moved = (iota((slots, slots), 0).astype(f32) == slot).astype(bf16)
    table = wide_sc[...]
    stack_sc[...] = jnp.zeros(stack_sc.shape, f32)
    stack_sc[0:SLOTS] = (table >> 8).astype(f32)
    stack_sc[SLOTS : 2 * SLOTS] = (table & 255).astype(f32)
    stack_sc[32:33] = (lane >> 8).astype(f32)
    stack_sc[33:34] = (lane & 255).astype(f32)
    for n, part in enumerate(thirds(place_ref[...])):
        at = 40 + n * TILE
        stack_sc[at : at + TILE, 0:owned] = part.astype(f32)
    turned = mm(stack_sc[...].astype(bf16), moved, NT)
    sorted_table = turned[0:SLOTS] * 256.0 + turned[SLOTS : 2 * SLOTS]
    table_out[...] = sorted_table.astype(jnp.int32)
    place_out[...] = (turned[40:48] + turned[48:56]) + turned[56:64]
    target = jnp.minimum(turned[32:33] * 256.0 + turned[33:34], owned - 1.0)
    for b in range(slots // LANES):
        part = target[:, b * LANES : (b + 1) * LANES]
        target_out[b : b + 1, :] = part.astype(jnp.int32) * TILE
    target_out[TILE:, :] = jnp.broadcast_to(total, (TILE, LANES)).astype(jnp.int32)

    def in_use_order(values, groups, out_ref):
        tall_sc[...] = jnp.zeros(tall_sc.shape, f32)
        for b in range(values.shape[1] // LANES):
            block = jnp.concatenate(
                [
                    values[:, b * LANES : (b + 1) * LANES],
                    jnp.zeros((LANES - values.shape[0], LANES), f32),
                ],
                axis=0,
            )
            tall_sc[b * LANES : (b + 1) * LANES, :] = block.T * 8.0
        rows = iota((LANES, LANES), 0)
        lanes = iota((LANES, LANES), 1)
        total = None
        for n in range(TILE):
            part = tall_sc[pl.ds(n, groups, TILE), :]
            high = jnp.floor(part * (1.0 / 256.0))
            low = part - high * 256.0
            place = (lanes == rows * TILE + n).astype(bf16)
            value = mm(high.astype(bf16), place) * 256.0 + mm(low.astype(bf16), place)
            total = value if total is None else total + value
        out_ref[...] = total.astype(jnp.int32)

    in_use_order(sorted_table, slots // TILE, flat_out)
    hubs = jnp.concatenate(
        [
            hub_table_ref[...].astype(f32),
            jnp.zeros((SLOTS - hub_table_ref.shape[0], LANES), f32),
        ],
        axis=0,
    )
    in_use_order(hubs, LANES // TILE, hub_out)


def order_atoms(table, hub_table, place):
    slots = up_to(table.shape[1], LANES)
    return pl.pallas_call(
        order_kernel,
        out_shape=(
            jax.ShapeDtypeStruct((SLOTS, slots), jnp.int32),
            jax.ShapeDtypeStruct((slots // TILE, LANES), jnp.int32),
            jax.ShapeDtypeStruct((LANES // TILE, LANES), jnp.int32),
            jax.ShapeDtypeStruct((2 * TILE, LANES), jnp.int32),
            jax.ShapeDtypeStruct((TILE, slots), f32),
        ),
        scratch_shapes=[
            pltpu.VMEM((SLOTS, slots), jnp.int32),
            pltpu.VMEM((64, slots), f32),
            pltpu.VMEM((slots, LANES), f32),
        ],
        compiler_params=pltpu.CompilerParams(vmem_limit_bytes=24 * MIB),
        name="order_atoms",
    )(table, hub_table, place)


def build_radial(wext32, wext, wr_ref, br_ref):
    width = wr_ref.shape[1] // 3
    orders = wr_ref.shape[0]
    wr = wr_ref[...].astype(f32)
    br = br_ref[...]
    bias_high = br.astype(bf16).astype(f32)
    bias_low = br - bias_high
    wext32[...] = jnp.zeros(wext32.shape, f32)
    for block, (row, column) in enumerate(
        ((0, 0), (0, 1), (1, 2), (2, 3), (3, 4))
    ):
        source = min(block, 2)
        at = row * ORDER_ROWS
        lanes = slice(column * width, (column + 1) * width)
        cols = slice(source * width, (source + 1) * width)
        wext32[at : at + orders, lanes] = wr[:, cols]
        wext32[at + orders : at + orders + 1, lanes] = bias_high[:, cols]
        wext32[at + orders + 1 : at + orders + 2, lanes] = bias_low[:, cols]
    wext[...] = wext32[...].astype(bf16)


def load_indices(idx_sc, tpos_sc, table_ref, target_ref):
    blocks = table_ref.shape[1] // LANES
    rows = idx_sc.shape[0]
    for b in range(blocks):
        at = b * SLOTS
        lanes = slice(b * LANES, (b + 1) * LANES)
        idx_sc[at : at + SLOTS, :] = table_ref[:, lanes]
        for c in range(3):
            tpos_sc[c * rows + at : c * rows + at + SLOTS, :] = jnp.broadcast_to(
                target_ref[c : c + 1, lanes], (SLOTS, LANES)
            )


def load_hubs(idx_sc, tpos_sc, hub_table_ref, hub_row_ref, place_sc, owned):
    rows = idx_sc.shape[0]
    at = rows - SLOTS
    idx_sc[at:, :] = jnp.zeros((SLOTS, LANES), jnp.int32)
    idx_sc[at : at + hub_table_ref.shape[0], :] = hub_table_ref[...]
    hub = jnp.broadcast_to(hub_row_ref[...], (TILE, LANES))
    lane = hub & (LANES - 1)
    chunk = hub >> 7
    total = jnp.zeros((TILE, LANES), f32)
    for t in range(-(-owned // LANES)):
        part = jnp.take_along_axis(
            place_sc[:, t * LANES : (t + 1) * LANES], lane, axis=1, mode="promise_in_bounds"
        )
        total = jnp.where(chunk == t, part, total)
    for c in range(3):
        tpos_sc[c * rows + at : c * rows + at + SLOTS, :] = jnp.broadcast_to(
            total[c : c + 1, :], (SLOTS, LANES)
        )


def geometry(idx, target, live, place_sc):
    lane = idx & (LANES - 1)
    chunk = idx >> 7
    chunks = place_sc.shape[1] // LANES
    offsets = []
    for c in range(3):
        total = jnp.zeros(idx.shape, f32)
        for t in range(chunks):
            table = jnp.broadcast_to(place_sc[c : c + 1, t * LANES : (t + 1) * LANES], idx.shape)
            part = jnp.take_along_axis(table, lane, axis=1, mode="promise_in_bounds")
            total = jnp.where(chunk == t, part, total)
        offsets.append(total - target[c])
    square = offsets[0] * offsets[0] + offsets[1] * offsets[1] + offsets[2] * offsets[2]
    distance = jnp.sqrt(jnp.where(live, square, 4.0))
    inverse = 1.0 / distance
    direction = [offset * inverse for offset in offsets]
    angle = (math.pi / CUTOFF) * distance
    sine = jnp.sin(angle)
    cosine = jnp.cos(angle)
    inside = live & (distance < CUTOFF)
    factor = jnp.where(inside, 0.5 * (cosine + 1.0), 0.0)
    slope = jnp.where(inside, (-0.5 * math.pi / CUTOFF) * sine, 0.0)
    return inverse, direction, sine, cosine, factor, slope


def fill_geometry(
    groups, blocks, owned, listed, hub_listed, hub_live, idx_sc, tpos_sc, place_sc, basis_sc, slope_sc, geo_sc, orders
):
    rows = idx_sc.shape[0]
    group = GROUP * SLOTS

    def step(i, carry):
        first = pl.multiple_of(i * group, SLOTS)

        def at(q):
            return pl.ds(pl.multiple_of(q * rows + first, SLOTS), group)

        row = iota((group, LANES), 0) + first
        block = row >> 4
        last = block == blocks
        valid = jnp.where(last, hub_live, owned - block * LANES)
        depth = jnp.where(last, hub_listed, listed)
        live = (iota((group, LANES), 1) < valid) & ((row & (SLOTS - 1)) < depth)
        inverse, direction, sine, cosine, factor, slope = geometry(
            idx_sc[pl.ds(first, group), :], [tpos_sc[at(c), :] for c in range(3)], live, place_sc
        )
        geo_sc[at(0), :] = factor
        for c in range(3):
            geo_sc[at(1 + c), :] = direction[c]
        geo_sc[at(4), :] = slope
        geo_sc[at(5), :] = inverse
        sine_n, cosine_n = sine, cosine
        for n in range(orders):
            ratio = sine_n * inverse
            basis_sc[at(n), :] = ratio.astype(bf16).astype(f32)
            if slope_sc is not None:
                slope_sc[at(n), :] = (((n + 1) * math.pi / CUTOFF) * cosine_n - ratio) * inverse
            if n + 1 < orders:
                sine_n, cosine_n = (
                    sine_n * cosine + cosine_n * sine,
                    cosine_n * cosine - sine_n * sine,
                )
        return carry

    lax.fori_loop(0, groups, step, 0)
    basis_sc[orders * rows : (orders + 2) * rows, :] = jnp.ones((2 * rows, LANES), f32)
    rest = (ORDER_ROWS - orders - 2) * rows
    basis_sc[(orders + 2) * rows :, :] = jnp.zeros((rest, LANES), f32)
    if slope_sc is not None:
        slope_sc[orders * rows :, :] = jnp.zeros((rest + 2 * rows, LANES), f32)


def unrolled(count, most):
    for size in range(most, 0, -1):
        if count % size == 0:
            return size
    return 1


def order_tiles(ref, row, rows):
    return [
        ref[pl.ds(row + t * TILE * rows, TILE, rows), :] for t in range(ORDER_ROWS // TILE)
    ]


def edge_coefficients(b, k, rows, basis_sc, geo_sc):
    row = b * SLOTS + k
    basis = order_tiles(basis_sc, row, rows)
    scale = [geo_sc[pl.ds(row + q * rows, 1), :] for q in range(4)]
    return basis, scale


def scaled_parts(basis, scale):
    plain = [part * scale[0] for part in basis]
    parts = []
    for c in range(3):
        parts += [part * scale[1 + c] for part in plain]
    return plain, parts


def make_filters(b, slots, rows, basis_sc, geo_sc, wext, filt, width):
    weights = wext[...]
    size = unrolled(slots, 5)
    for first in range(0, slots, size):
        turned = []
        for k in range(first, first + size):
            basis, scale = edge_coefficients(b, k, rows, basis_sc, geo_sc)
            plain, parts = scaled_parts(basis, scale)
            turned.append(jnp.concatenate(plain + parts, axis=0).T.astype(bf16))
        store_filters(first, turned, weights, filt, width)


def put_slot(filt, k, slot, value):
    filt[:, pl.ds(k * TILE * STEP + slot, TILE, STEP), :] = value.reshape(-1, TILE, LANES)


def get_slot(filt, k, slot):
    return filt[:, pl.ds(k * TILE * STEP + slot, TILE, STEP), :].reshape(LANES, LANES)


def store_filters(first, coeffs, weights, filt, width):
    product = mm(jnp.concatenate(coeffs, axis=0), weights)
    for n in range(len(coeffs)):
        for slot in range(7):
            column = 0 if slot < 3 else slot - 2
            put_slot(
                filt,
                first + n,
                slot,
                product[n * LANES : (n + 1) * LANES, column * width : (column + 1) * width],
            )


def fill_filters(slots, turned_sc, wext, filt, width, extra):
    weights = wext[...]
    size = unrolled(slots, 5)
    for first in range(0, slots, size):
        coeff = [turned_sc[k * LANES : (k + 1) * LANES, :] for k in range(first, first + size)]
        store_filters(first, coeff, weights, filt, width)
        for k in range(first, first + size):
            put_slot(filt, k, 7, extra(k))


def sigmoid(t):
    return 1.0 / (1.0 + jnp.exp(-t))


def message_net(rows, w1, b1, w2, b2):
    lead = rows[:, 0:LANES].astype(bf16)
    pre = mm(lead, w1) + b1
    gate = sigmoid(pre)
    hidden = (pre * gate).astype(bf16)
    filters = (mm(hidden, w2) + b2).astype(bf16).astype(f32)
    return lead, pre, gate, hidden, filters


def store_table(tiles, firsts, counts, rows, filters):
    gate = filters[:, 0:LANES]
    columns = [rows[:, (1 + c) * LANES : (2 + c) * LANES] * gate for c in range(3)]
    columns += [filters[:, LANES : 2 * LANES]] + [filters[:, 2 * LANES :]] * 3
    at = 0
    for first, count in zip(firsts, counts):
        for slot, column in enumerate(columns):
            tiles[pl.ds(first * TILE + slot, count, TILE), :] = column[at : at + count, :]
        at += count


def build_table(tiles, halo, arrived, w1, b1, w2, b2):
    counts = [up_to(h[1], TILE) for h in halo]
    firsts = [h[0] for h in halo]
    sides = jnp.concatenate([ref[0:count, :] for count, ref in zip(counts, arrived)], axis=0)
    store_table(tiles, firsts, counts, sides, message_net(sides, w1, b1, w2, b2)[4])


def tile_at(ref, row):
    return ref[pl.ds(pl.multiple_of(row * TILE, TILE), TILE), :]


def edge_at(k, n):
    return pl.ds((k * TILE + n) * STEP, TILE)


def source_at(ref, row):
    return ref[pl.ds(pl.multiple_of(row, TILE), TILE), :]


def sum_group(filt, tiles, flat, targets, sums, b, i, listed):
    first = b * LANES + i * TILE
    for n in range(TILE):
        total = None
        for k in range(listed):
            source = flat[first * SLOTS + k * TILE + n]
            part = source_at(tiles, source) * filt[i, edge_at(k, n), :]
            total = part if total is None else total + part
        sums[pl.ds(pl.multiple_of(targets[first + n], TILE), TILE), :] = total


def inner_kernel(
    listed,
    flat,
    targets,
    rows_ref,
    p_ref,
    table_ref,
    target_ref,
    w1_ref,
    b1_ref,
    w2_ref,
    b2_ref,
    wr_ref,
    br_ref,
    sums,
    tiles,
    filt,
    place_sc,
    idx_sc,
    tpos_sc,
    basis_sc,
    geo_sc,
    wext32,
    wext,
):
    owned = rows_ref.shape[0]
    orders = wr_ref.shape[0]
    rows = idx_sc.shape[0]
    place_sc[...] = jnp.zeros(place_sc.shape, f32)
    place_sc[:, 0:owned] = p_ref[...]
    build_radial(wext32, wext, wr_ref, br_ref)
    load_indices(idx_sc, tpos_sc, table_ref, target_ref)
    done = targets[TILE * LANES] // TILE
    each = LANES // TILE
    blocks = (done + each - 1) // each
    fill_geometry(
        (blocks + GROUP - 1) // GROUP,
        rows // SLOTS,
        owned,
        listed,
        0,
        0,
        idx_sc,
        tpos_sc,
        place_sc,
        basis_sc,
        None,
        geo_sc,
        orders,
    )
    own = rows_ref[...]
    weights = (w1_ref[...], b1_ref[...], w2_ref[...], b2_ref[...])
    store_table(tiles, [0], [owned], own, message_net(own, *weights)[4])
    sums[...] = jnp.zeros(sums.shape, f32)

    def regular_block(b, carry):
        make_filters(b, listed, rows, basis_sc, geo_sc, wext, filt, LANES)

        def atoms(i, inner):
            sum_group(filt, tiles, flat, targets, sums, b, i, listed)
            return inner

        lax.fori_loop(0, jnp.minimum(each, done - b * each), atoms, 0)
        return carry

    lax.fori_loop(0, blocks, regular_block, 0)


def forward_kernel(
    halo,
    shapes,
    listed,
    hub_listed,
    chunk,
    size_y,
    flat_table,
    flat_hub_table,
    targets,
    hub_list,
    hub_count,
    place_y,
    rows_ref,
    p_ref,
    cot_ref,
    table_ref,
    target_ref,
    hub_table_ref,
    hub_row_ref,
    sums_in,
    w1_ref,
    b1_ref,
    w2_ref,
    b2_ref,
    wr_ref,
    br_ref,
    u_ref,
    v_ref,
    w3_ref,
    b3_ref,
    w4_ref,
    b4_ref,
    *rest,
):
    arrived, rest = arrived_views([h[1] for h in halo[::2]], shapes, rest)
    (
        out_s_ref,
        out_v_ref,
        grad_ref,
        bias_ref,
        tiles,
        basis_sc,
        slope_sc,
        geo_sc,
    ) = rest[:8]
    share_refs = rest[8 : 8 + size_y]
    (
        filt,
        sums,
        place_sc,
        idx_sc,
        tpos_sc,
        wext32,
        wext,
        uv,
        out_sc,
        early_ref,
    ) = rest[8 + size_y :]
    owned = rows_ref.shape[0]
    width = LANES
    orders = wr_ref.shape[0]
    blocks = -(-owned // LANES)
    build_places(place_sc, p_ref, owned, halo, arrived)
    build_radial(wext32, wext, wr_ref, br_ref)
    load_indices(idx_sc, tpos_sc, table_ref, target_ref)
    load_hubs(idx_sc, tpos_sc, hub_table_ref, hub_row_ref, place_sc, owned)
    hub_live = hub_count[0]
    fill_geometry(
        -(-(blocks + 1) // GROUP), blocks, owned, listed, hub_listed, hub_live, idx_sc, tpos_sc, place_sc, basis_sc, slope_sc, geo_sc, orders
    )
    rows = idx_sc.shape[0]
    sums[...] = sums_in[...]
    weights = (w1_ref[...], b1_ref[...], w2_ref[...], b2_ref[...])
    own = rows_ref[...]
    store_table(tiles, [0], [owned], own, message_net(own, *weights)[4])
    build_table(tiles, halo, arrived, *weights)
    done = targets[TILE * LANES] // TILE
    each = LANES // TILE

    def regular_block(b, carry):
        make_filters(b, listed, rows, basis_sc, geo_sc, wext, filt, width)

        def atoms(i, inner):
            sum_group(filt, tiles, flat_table, targets, sums, b, i, listed)
            return inner

        def pairs(i, inner):
            for part in range(2):
                sum_group(filt, tiles, flat_table, targets, sums, b, 2 * i + part, listed)
            return inner

        start = jnp.maximum(done - b * each, 0)
        end = jnp.minimum(each, owned // TILE - b * each)
        lax.fori_loop(start // 2, end // 2, pairs, 0)
        lax.fori_loop(end // 2 * 2, end, atoms, 0)
        return carry

    lax.fori_loop(done // each, blocks, regular_block, 0)
    make_filters(blocks, min(listed, up_to(hub_listed, 4)), rows, basis_sc, geo_sc, wext, filt, width)

    def hub_slots(i, carry):
        for n in range(TILE):
            total = None
            for k in range(hub_listed):
                source = flat_hub_table[i * LANES + k * TILE + n]
                part = source_at(tiles, source) * filt[i, edge_at(k, n), :]
                total = part if total is None else total + part
            at = pl.ds(pl.multiple_of(hub_list[i * TILE + n] * TILE, TILE), TILE)
            sums[at, :] = sums[at, :] + total
        return carry

    lax.fori_loop(0, (hub_live + TILE - 1) // TILE, hub_slots, 0)

    uv[:, 0:width] = u_ref[...]
    uv[:, width:] = v_ref[...]
    early_ref[...] = jnp.zeros(early_ref.shape, f32)
    bias_ref[...] = jnp.zeros(bias_ref.shape, f32)

    def update(i, carry):
        first = pl.multiple_of(i * chunk, TILE)
        part = [sums[pl.ds(first * TILE + slot, chunk, TILE), :] for slot in range(7)]
        own = rows_ref[pl.ds(first, chunk), :]
        cot = cot_ref[pl.ds(first, chunk), :]
        state_s = own[:, 0:width] + part[3]
        state_v = [
            own[:, (1 + c) * width : (2 + c) * width] + (part[c] + part[4 + c]) for c in range(3)
        ]
        low = [x.astype(bf16) for x in state_v]
        both = [mm(x, uv[...]) for x in low]
        left = [x[:, 0:width] for x in both]
        right = [x[:, width:] for x in both]
        inner = left[0] * right[0] + left[1] * right[1] + left[2] * right[2]
        norm = jnp.sqrt(right[0] * right[0] + right[1] * right[1] + right[2] * right[2] + 1.0)
        joined = jnp.concatenate([state_s, norm], axis=1).astype(bf16)
        pre = mm(joined, w3_ref[...]) + b3_ref[...]
        gate = sigmoid(pre)
        hidden = (pre * gate).astype(bf16)
        amp = mm(hidden, w4_ref[...]) + b4_ref[...]
        amp_vv = amp[:, 0:width]
        amp_sv = amp[:, width : 2 * width]
        amp_ss = amp[:, 2 * width :]
        out_sc[pl.ds(first, chunk), 0:width] = state_s + amp_sv * inner + amp_ss
        for c in range(3):
            out_sc[pl.ds(first, chunk), (1 + c) * width : (2 + c) * width] = (
                state_v[c] + amp_vv * left[c]
            )
        gs = cot[:, 0:width]
        gv = [cot[:, (1 + c) * width : (2 + c) * width] for c in range(3)]
        grad_amp = jnp.concatenate(
            [gv[0] * left[0] + gv[1] * left[1] + gv[2] * left[2], gs * inner, gs], axis=1
        )
        grad_amp_low = grad_amp.astype(bf16)
        grad_w4 = mm(hidden, grad_amp_low, TN)
        for t in range(3):
            early_ref[(4 + t) * width : (5 + t) * width, :] += grad_w4[:, t * width : (t + 1) * width]
            bias_ref[1 + t : 2 + t, :] += jnp.sum(
                grad_amp[:, t * width : (t + 1) * width], axis=0, keepdims=True
            )
        slope = gate * (1.0 + pre * (1.0 - gate))
        grad_pre = mm(grad_amp_low, w4_ref[...], NT) * slope
        bias_ref[0:1, :] += jnp.sum(grad_pre, axis=0, keepdims=True)
        grad_pre_low = grad_pre.astype(bf16)
        early_ref[2 * width : 4 * width, :] += mm(joined, grad_pre_low, TN)
        grad_joined = mm(grad_pre_low, w3_ref[...], NT)
        mixed = gs * amp_sv
        ratio = grad_joined[:, width:] / norm
        grad_ref[pl.ds(first * TILE + 3, chunk, TILE), :] = gs + grad_joined[:, 0:width]
        grad_ref[pl.ds(first * TILE + 7, chunk, TILE), :] = jnp.ones((chunk, width), f32)
        grad_uv = None
        for c in range(3):
            grad_left = gv[c] * amp_vv + mixed * right[c]
            grad_right = mixed * left[c] + ratio * right[c]
            grad_both = jnp.concatenate([grad_left, grad_right], axis=1).astype(bf16)
            piece = mm(low[c], grad_both, TN)
            grad_uv = piece if grad_uv is None else grad_uv + piece
            grad_v = gv[c] + mm(grad_both, uv[...], NT)
            grad_ref[pl.ds(first * TILE + c, chunk, TILE), :] = grad_v
            grad_ref[pl.ds(first * TILE + 4 + c, chunk, TILE), :] = grad_v
        early_ref[0:width, :] += grad_uv[:, 0:width]
        early_ref[width : 2 * width, :] += grad_uv[:, width:]
        return carry

    lax.fori_loop(0, owned // chunk, update, 0)
    out_s_ref[...] = out_sc[:, 0:width].astype(bf16)
    out_v_ref[...] = out_sc[:, width:].astype(bf16)
    give_shares(place_y[0], early_ref, share_refs)


def places_of(sums, first, count):
    select = (iota((TILE, LANES), 0) == (iota((TILE, LANES), 1) & 7)).astype(bf16)
    value = sums[pl.ds(first * TILE + 7, count, TILE), :]
    high, middle, low = thirds(value)
    return (mm(select, high, NT) + mm(select, middle, NT)) + mm(select, low, NT)


def message_back(late_ref, weights, rows, part, own_grads):
    w1, b1, w2, b2 = weights
    width = LANES
    bias_at = 4 * width + 3 * ORDER_ROWS
    lead, pre, gate, hidden, filters = message_net(rows, w1, b1, w2, b2)
    vec = [rows[:, (1 + c) * width : (2 + c) * width] for c in range(3)]
    grad_filters = jnp.concatenate(
        [
            vec[0] * part[0] + vec[1] * part[1] + vec[2] * part[2],
            part[3],
            part[4] + part[5] + part[6],
        ],
        axis=1,
    )
    low = grad_filters.astype(bf16)
    grad_w2 = mm(hidden, low, TN)
    for t in range(3):
        late_ref[(1 + t) * width : (2 + t) * width, :] += grad_w2[:, t * width : (t + 1) * width]
        at = bias_at + 1 + t
        late_ref[at : at + 1, :] += jnp.sum(
            grad_filters[:, t * width : (t + 1) * width], axis=0, keepdims=True
        )
    grad_pre = mm(low, w2, NT) * (gate * (1.0 + pre * (1.0 - gate)))
    late_ref[bias_at : bias_at + 1, :] += jnp.sum(grad_pre, axis=0, keepdims=True)
    grad_pre_low = grad_pre.astype(bf16)
    late_ref[0:width, :] += mm(lead, grad_pre_low, TN)
    gate_vv = filters[:, 0:width]
    grads = [mm(grad_pre_low, w1, NT)] + [gate_vv * part[c] for c in range(3)]
    if own_grads is None:
        return grads
    return [x + y for x, y in zip(grads, own_grads)]


def backward_kernel(
    halo,
    shapes,
    listed,
    hub_listed,
    flat_table,
    flat_hub_table,
    targets,
    hub_list,
    hub_count,
    grads,
    bias_ref,
    tiles,
    basis_sc,
    slope_sc,
    geo_sc,
    w1_ref,
    b1_ref,
    w2_ref,
    b2_ref,
    wr_ref,
    br_ref,
    *rest,
):
    arrived, rest = arrived_views([h[1] for h in halo[::2]], shapes, rest)
    sums, target_sc, late_ref = rest[:3]
    rest = rest[3:]
    packets = rest[4 : 4 + shapes[2]]
    side_refs = list(rest[:4]) + pair_views(packets, packed_rows(halo[4][1]))
    rest = rest[4 + shapes[2] :]
    (
        filt,
        wext32,
        wext,
        turned_sc,
        coeff_sc,
        mix_sc,
        reduce_sc,
        spread_sc,
        radial_sc,
    ) = rest
    owned = grads.shape[0] // TILE
    width = LANES
    orders = wr_ref.shape[0]
    blocks = -(-owned // LANES)
    build_radial(wext32, wext, wr_ref, br_ref)
    hub_live = hub_count[0]
    rows = geo_sc.shape[0] // 6
    weights = (w1_ref[...], b1_ref[...], w2_ref[...], b2_ref[...])
    sums[...] = jnp.zeros(sums.shape, f32)
    radial_sc[...] = jnp.zeros(radial_sc.shape, f32)
    spread_sc[...] = jnp.zeros(spread_sc.shape, f32)
    reduce_sc[...] = jnp.zeros(reduce_sc.shape, f32)
    late_ref[...] = jnp.zeros(late_ref.shape, f32)

    def block_grads(b, count, trips, source_of, target_of):
        def mixes(pair, inner):
            for part in range(2):
                i = pair * 2 + part
                for n in range(TILE):
                    grad = source_at(grads, target_of(i, n))
                    for k in range(count):
                        filt[i, edge_at(k, n), :] = grad * source_at(tiles, source_of(i, k, n))
            return inner

        lax.fori_loop(0, trips, mixes, 0)
        span = min(listed, up_to(count, 4)) if count != listed else listed
        size = unrolled(span, 5)
        step = size * LANES

        def analyse(i, carry):
            first = i * step
            loaded = []
            for n in range(size):
                k = i * size + n
                part = [get_slot(filt, k, slot) for slot in range(7)]
                at = pl.ds(k * LANES, LANES)
                mix = [part[0] + part[1] + part[2], part[3], part[4], part[5], part[6]]
                for q in range(5):
                    mix_sc[at, q * width : (q + 1) * width] = mix[q].astype(bf16)
                row = b * SLOTS + k
                basis, scale = edge_coefficients(b, k, rows, basis_sc, geo_sc)
                loaded.append((basis, scale, order_tiles(slope_sc, row, rows)))
                plain, parts = scaled_parts(basis, scale)
                coeff = jnp.concatenate(plain + parts, axis=0)
                coeff_sc[:, at] = coeff.astype(bf16)
                turned_sc[at, :] = coeff.T.astype(bf16)
            mixes = mix_sc[pl.ds(first, step), :]
            backs = mm(wext[...], mixes, NT)
            radial_sc[...] += mm(coeff_sc[:, pl.ds(first, step)], mixes)
            for n, (basis, scale, slopes) in enumerate(loaded):
                back = backs[:, n * LANES : (n + 1) * LANES]
                total = None
                for t in range(ORDER_ROWS // TILE):
                    pieces = [
                        back[j * ORDER_ROWS + t * TILE : j * ORDER_ROWS + (t + 1) * TILE, :]
                        for j in range(4)
                    ]
                    mixed = (
                        pieces[0]
                        + pieces[1] * scale[1]
                        + pieces[2] * scale[2]
                        + pieces[3] * scale[3]
                    )
                    values = [mixed * basis[t], mixed * slopes[t]] + [
                        pieces[1 + c] * basis[t] for c in range(3)
                    ]
                    total = values if total is None else [x + y for x, y in zip(total, values)]
                for q in range(5):
                    at = q * TILE * SLOTS + i * size + n
                    reduce_sc[pl.ds(at, TILE, SLOTS), :] = total[q]
            return carry

        for i in range(span // size):
            analyse(i, 0)

        def geo(q):
            return geo_sc[pl.ds(pl.multiple_of(q * rows + b * SLOTS, SLOTS), SLOTS), :]

        factor = geo(0)
        direction = [geo(1 + c) for c in range(3)]
        slope = geo(4)
        inverse = geo(5)
        red = []
        for q in range(5):
            at = q * TILE * SLOTS
            pieces = [reduce_sc[at + n * SLOTS : at + (n + 1) * SLOTS] for n in range(TILE)]
            red.append(sum(pieces[1:], pieces[0]))
        grad_d = factor * red[1] + slope * red[0]
        grad_u = [factor * red[2 + c] for c in range(3)]
        along = (
            direction[0] * grad_u[0] + direction[1] * grad_u[1] + direction[2] * grad_u[2]
        )
        row = iota((SLOTS, LANES), 0)
        for c in range(3):
            value = (grad_u[c] - direction[c] * along) * inverse + grad_d * direction[c]
            value = jnp.where(row < count, value, 0.0)
            spread_sc[pl.ds(c, SLOTS, TILE), :] = value
            target_sc[b, c : c + 1, :] = -jnp.sum(value, axis=0, keepdims=True)
        turned = spread_sc[...].T
        group_of = iota((LANES, LANES), 1) >> 3
        fill_filters(
            span, turned_sc, wext, filt, width, lambda k: jnp.where(group_of == k, turned, 0.0)
        )

        def scatter(pair, inner):
            for part in range(2):
                i = pair * 2 + part
                for n in range(TILE):
                    grad = source_at(grads, target_of(i, n))
                    places = [
                        pl.ds(pl.multiple_of(source_of(i, k, n), TILE), TILE)
                        for k in range(count)
                    ]
                    held = [sums[at, :] for at in places]
                    fresh = [held[k] + grad * filt[i, edge_at(k, n), :] for k in range(count)]
                    for k in range(count):
                        sums[places[k], :] = fresh[k]
            return inner

        lax.fori_loop(0, trips, scatter, 0)

    target_sc[...] = jnp.zeros(target_sc.shape, f32)

    def regular_block(b, carry):
        base = b * LANES
        block_grads(
            b,
            listed,
            (jnp.minimum(LANES, owned - base) + 2 * TILE - 1) // (2 * TILE),
            lambda i, k, n: flat_table[(base + i * TILE) * SLOTS + k * TILE + n],
            lambda i, n: targets[base + i * TILE + n],
        )
        return carry

    lax.fori_loop(0, blocks, regular_block, 0)
    block_grads(
        blocks,
        hub_listed,
        (hub_live + 2 * TILE - 1) // (2 * TILE),
        lambda i, k, n: flat_hub_table[i * LANES + k * TILE + n],
        lambda i, n: hub_list[i * TILE + n] * TILE,
    )

    bias_at = 4 * width + 3 * ORDER_ROWS
    side_parts = []
    for first, count, _, _ in halo:
        count8 = up_to(count, TILE)
        part = [sums[pl.ds(first * TILE + slot, count8, TILE), :] for slot in range(7)]
        if count8 != count:
            keep = iota((count8, 1), 0) < count
            part = [jnp.where(keep, x, 0.0) for x in part]
        side_parts.append(part)
    side_rows = jnp.concatenate(
        [ref[0 : up_to(h[1], TILE), :] for h, ref in zip(halo, arrived)], axis=0
    )
    side_grads = message_back(
        late_ref, weights, side_rows, [jnp.concatenate(x, axis=0) for x in zip(*side_parts)], None
    )
    at = 0
    for index, (first, count, _, _) in enumerate(halo):
        count8 = up_to(count, TILE)
        side_ref = side_refs[index]
        side_ref[...] = jnp.zeros(side_ref.shape, f32)
        for q in range(4):
            side_ref[0:count8, q * width : (q + 1) * width] = side_grads[q][at : at + count8, :]
        at += count8
        write_places(side_ref, count, places_of(sums, first, count))

    for t in range(3):
        if t < 2:
            value = radial_sc[0:orders, t * width : (t + 1) * width]
            bias = radial_sc[orders : orders + 1, t * width : (t + 1) * width]
        else:
            value = None
            bias = None
            for c in range(3):
                at = (1 + c) * ORDER_ROWS
                lanes = slice((2 + c) * width, (3 + c) * width)
                one = radial_sc[at : at + orders, lanes]
                two = radial_sc[at + orders : at + orders + 1, lanes]
                value = one if value is None else value + one
                bias = two if bias is None else bias + two
        late_ref[4 * width + t * ORDER_ROWS : 4 * width + t * ORDER_ROWS + orders, :] = value
        late_ref[bias_at + 4 + t : bias_at + 5 + t, :] = bias

    late_ref[bias_at + 7 : bias_at + 11, :] = bias_ref[0:4, :]


def own_back_kernel(
    shares,
    me,
    sums,
    target_ref,
    late_in,
    s_ref,
    v_ref,
    grads,
    names_ref,
    hub_row_ref,
    w1_ref,
    b1_ref,
    w2_ref,
    b2_ref,
    *rest,
):
    early, rest = rest[:shares], rest[shares:]
    own_ref, place_ref, early_ref = rest[:3]
    share_refs, late_ref = rest[3:-1], rest[-1]
    early_ref[...] = summed(early)
    owned = s_ref.shape[0]
    rows = jnp.concatenate([s_ref[...].astype(f32), v_ref[...].astype(f32)], axis=1)
    width = LANES
    hubs = hub_row_ref.shape[1]
    blocks = -(-owned // LANES)
    weights = (w1_ref[...], b1_ref[...], w2_ref[...], b2_ref[...])
    late_ref[...] = late_in[...]
    parts = [sums[pl.ds(slot, owned, TILE), :] for slot in range(7)]
    held = [grads[pl.ds(slot, owned, TILE), :] for slot in (3, 0, 1, 2)]
    own_grads = message_back(late_ref, weights, rows, parts, held)
    for q in range(4):
        own_ref[:, q * width : (q + 1) * width] = own_grads[q]
    give_shares(me[0], late_ref, share_refs)
    place_ref[...] = places_of(sums, 0, owned)
    total = None
    for b in range(blocks + 1):
        names = hub_row_ref[...] * TILE if b == blocks else names_ref[b : b + 1, :]
        onehot = (iota((owned, hubs), 0) * TILE == jnp.broadcast_to(names, (owned, hubs))).astype(bf16)
        part = pick_exact(target_ref[b], onehot)
        total = part if total is None else total + part
    place_ref[...] += total


def chunk_of(ref, me, shift, count):
    size = ref.shape[0] // count
    at = lax.rem(me + shift, count) * size
    return ref[pl.ds(pl.multiple_of(at, TILE), size), :]


def give_shares(me, ref, share_refs):
    for t, share_ref in enumerate(share_refs):
        share_ref[...] = chunk_of(ref, me, t, len(share_refs))


def gathered_back(first, count, pieces):
    rows = sum(list_ref.shape[1] for _, list_ref, _ in pieces)
    target = iota((count, rows), 0) + first
    names = jnp.concatenate(
        [
            jnp.broadcast_to(list_ref[side : side + 1, :], (TILE, list_ref.shape[1]))
            for _, list_ref, side in pieces
        ],
        axis=1,
    )
    onehot = (target == names[0:1, :]).astype(bf16)
    values = jnp.concatenate(
        [ref[0 : list_ref.shape[1], :] for ref, list_ref, _ in pieces], axis=0
    ).astype(bf16)
    places = jnp.concatenate(
        [read_places(ref, list_ref.shape[1])[:, 0 : list_ref.shape[1]] for ref, list_ref, _ in pieces],
        axis=1,
    )
    return mm(onehot, values), pick_exact(places, onehot)


def list_pieces(lists, arrived):
    pieces = []
    for n, list_ref in enumerate(lists):
        pieces += [(arrived[2 * n], list_ref, 0), (arrived[2 * n + 1], list_ref, 1)]
    return pieces


def add_back(first, count, pieces, part_ref, out_ref):
    count8 = up_to(count, TILE)
    total, places = gathered_back(first, count8, pieces)
    if count8 != count:
        total = jnp.where(iota((count8, 1), 0) < count, total, 0.0)
    rows = part_ref.shape[0]
    out_ref[0:rows, :] = part_ref[...]
    out_ref[0:count8, :] += total
    write_places(out_ref, count, read_places(part_ref, count)[:, 0:count] + places[:, 0:count])


def return_y_kernel(ranges, sizes, me, z_list, *refs):
    size_z, size_y = sizes
    z_size = 1 if size_z == 2 else 2
    y_size = 1 if size_y == 2 else 2
    packets, refs = refs[:z_size], refs[z_size:]
    late, refs = refs[:size_y], refs[size_y:]
    early, refs = refs[0], refs[1:]
    partial, refs = refs[:2], refs[2:]
    outs, refs = refs[:y_size], refs[y_size:]
    share_refs, share = refs[:-1], refs[-1]
    size = late[0].shape[0]
    share[0:size, :] = summed(late)
    share[size:, :] = early[...]
    give_shares(me[0], share, share_refs)
    arrived, _ = arrived_views([z_list.shape[1]], [z_size], packets)
    pieces = list_pieces([z_list], arrived)
    y_rows = packed_rows(ranges[0][1])
    for (first, count), part_ref, out_ref in zip(ranges, partial, pair_views(outs, y_rows)):
        add_back(first, count, pieces, part_ref, out_ref)


def return_x_kernel(ranges, sizes, z_list, y_list, *refs):
    size_z, size_y = sizes
    shapes = [1 if size == 2 else 2 for size in sizes]
    arrived, rest = arrived_views([z_list.shape[1], y_list.shape[1]], shapes, refs)
    shares, rest = rest[:size_z], rest[size_z:]
    partial, rest = rest[:2], rest[2:]
    outs, keep_x = rest[:-1], rest[-1]
    keep_x[...] = summed(shares)
    x_rows = packed_rows(ranges[0][1])
    pieces = list_pieces([z_list, y_list], arrived)
    for (first, count), part_ref, out_ref in zip(ranges, partial, pair_views(outs, x_rows)):
        add_back(first, count, pieces, part_ref, out_ref)


def own_kernel(shapes, *refs):
    phases = len(shapes)
    lists = refs[:phases]
    arrived, rest = arrived_views([x.shape[1] for x in lists], shapes, refs[phases:])
    own_ref, place_ref, *outs = rest
    total, places = gathered_back(0, own_ref.shape[0], list_pieces(lists, arrived))
    total = total + own_ref[...]
    places = places + place_ref[...]
    if len(outs) == 2:
        outs[0][...] = total
        outs[1][...] = places
    else:
        outs[0][...] = total[:, 0:LANES]
        outs[1][...] = total[:, LANES:]
        outs[2][...] = places[0:3, :]


def summed(refs):
    total = refs[0][...]
    for ref in refs[1:]:
        total = total + ref[...]
    return total


def sum_kernel(*refs):
    refs[-1][...] = summed(refs[:-1])


def join_kernel(me, *refs):
    shares, out_ref = refs[:-1], refs[-1]
    count = len(shares)
    size = shares[0].shape[0]
    for t in range(count):
        at = lax.rem(me[0] + count - t, count) * size
        out_ref[pl.ds(pl.multiple_of(at, TILE), size), :] = shares[t][...]


def gather_order(me, count):
    if count != 4:
        return [lax.rem(me + count - t, count) for t in range(count)]
    beside = me + 1 - 2 * lax.rem(me, 2)
    return [me, beside, lax.rem(me + 2, 4), lax.rem(beside + 2, 4)]


def unpack_kernel(sizes, late_share, me, *refs):
    size_y, size_z = sizes
    late_ref, early_ref, joined = refs[-3:]
    outs = refs[size_y:-3]
    share = late_share + early_ref.shape[0] // size_y
    for t, owner in enumerate(gather_order(me[0], size_y)):
        joined[pl.ds(pl.multiple_of(owner * share, TILE), share), :] = refs[t][...]
    rest = share - late_share
    for n in range(size_y):
        late_ref[n * late_share : (n + 1) * late_share, :] = joined[
            n * share : n * share + late_share, :
        ]
        early_ref[n * rest : (n + 1) * rest, :] = joined[n * share + late_share : (n + 1) * share, :]
    (w1, b1, w2, b2, wr, br, u, v, w3, b3, w4, b4) = outs
    width = LANES
    orders = wr.shape[0]
    bias_at = 4 * width + 3 * ORDER_ROWS
    u[...] = early_ref[0:width, :]
    v[...] = early_ref[width : 2 * width, :]
    w3[...] = early_ref[2 * width : 4 * width, :]
    b3[...] = late_ref[bias_at + 7, :]
    w1[...] = late_ref[0:width, :]
    b1[...] = late_ref[bias_at, :]
    for t in range(3):
        lanes = slice(t * width, (t + 1) * width)
        w4[:, lanes] = early_ref[(4 + t) * width : (5 + t) * width, :]
        b4[lanes] = late_ref[bias_at + 8 + t, :]
        w2[:, lanes] = late_ref[(1 + t) * width : (2 + t) * width, :]
        b2[lanes] = late_ref[bias_at + 1 + t, :]
        at = 4 * width + t * ORDER_ROWS
        wr[:, lanes] = late_ref[at : at + orders, :]
        br[lanes] = late_ref[bias_at + 4 + t, :]


def work(array, operations):
    return pl.CostEstimate(
        flops=operations, bytes_accessed=4 * array.size * array.dtype.itemsize, transcendentals=0
    )


def exchange(axis, packets):
    count = lax.axis_size(axis)
    up = [(i, (i + 1) % count) for i in range(count)]
    if len(packets) == 1:
        return [lax.ppermute(packets[0], axis, up)]
    down = [(j, i) for i, j in up]
    return [lax.ppermute(packets[1], axis, up), lax.ppermute(packets[0], axis, down)]


def rotated(axis, pieces):
    count = lax.axis_size(axis)
    return [pieces[0]] + [
        lax.ppermute(pieces[t], axis, [(i, (i + t) % count) for i in range(count)])
        for t in range(1, count)
    ]


def gathered(axis, piece):
    if lax.axis_size(axis) != 4:
        return rotated(axis, [piece] * lax.axis_size(axis))
    beside = [(i, i ^ 1) for i in range(4)]
    across = lax.ppermute(piece, axis, [(i, (i + 2) % 4) for i in range(4)])
    near = lax.ppermute(piece, axis, beside)
    return [piece, near, across, lax.ppermute(across, axis, beside)]


def local(
    scalar_feat,
    vector_feat,
    positions,
    message_inner,
    message_inner_bias,
    message_outer,
    message_outer_bias,
    radial_weight,
    radial_bias,
    update_left,
    update_right,
    update_inner,
    update_inner_bias,
    update_outer,
    update_outer_bias,
    scalar_cotangent,
    vector_cotangent,
    x_face_rows,
    y_face_rows,
    z_face_rows,
    neighbour_table,
    hub_atoms,
    hub_table,
    hub_count,
):
    owned, width = scalar_feat.shape
    length = G * SPACING
    counts = [x_face_rows.shape[2], y_face_rows.shape[2], z_face_rows.shape[2]]
    lists = [x_face_rows[0], y_face_rows[0], z_face_rows[0]]
    axes = ("gx", "gy", "gz")
    halo = []
    first = owned
    for number, count in enumerate(counts):
        halo.append((first, count, number, -length))
        halo.append((first + count, count, number, length))
        first += 2 * count
    ext = first
    packets, (rows, place, y_list, z_list) = first_pack(
        axes[0], lists, scalar_feat, vector_feat, positions
    )
    lists = [lists[0], y_list, z_list]
    arrived = exchange(axes[0], packets)
    shapes = [len(packets)]
    own_packs = pack_own(lists[1:], rows, place)
    table, flat_table, flat_hub_table, names, target_place = order_atoms(
        neighbour_table, hub_table, place
    )
    for number in range(1, 3):
        own = own_packs[2 * number - 2 : 2 * number]
        packets = pack_sides(
            axes[number], lists[number], own, halo[: 2 * number], shapes, arrived
        )
        packets, names = lax.optimization_barrier((packets, names))
        arrived = arrived + exchange(axes[number], packets)
        shapes.append(len(packets))
    shapes = tuple(shapes)

    cots = jnp.concatenate([scalar_cotangent, vector_cotangent], axis=1).astype(f32)
    flat_table = flat_table.reshape(-1)
    flat_hub_table = flat_hub_table.reshape(-1)
    targets = names.reshape(-1)
    hub_row = hub_atoms.reshape(1, -1)
    b1 = message_inner_bias.reshape(1, -1)
    b2 = message_outer_bias.reshape(1, -1)
    br = radial_bias.reshape(1, -1)
    b3 = update_inner_bias.reshape(1, -1)
    b4 = update_outer_bias.reshape(1, -1)

    blocks = -(-owned // LANES)
    chunk = owned
    ext_tiles = up_to(ext, TILE) * TILE
    slots = neighbour_table.shape[0]
    assert slots <= SLOTS and hub_table.shape[0] <= slots and owned % TILE == 0
    assert hub_atoms.shape[0] == LANES and blocks <= TILE
    hub_slots = hub_table.shape[0]
    inner_rows = up_to(blocks, GROUP) * SLOTS
    smem = pl.BlockSpec(memory_space=pltpu.SMEM)
    vmem = pl.BlockSpec(memory_space=pltpu.VMEM)
    small = pltpu.CompilerParams(vmem_limit_bytes=8 * MIB)
    middle = pltpu.CompilerParams(vmem_limit_bytes=20 * MIB)
    wide = 5 * width
    size_x, size_y, size_z = [lax.axis_size(axis) for axis in axes]
    step = TILE * size_y * size_z
    late_rows = up_to(4 * width + 3 * ORDER_ROWS + 2 * TILE, step)
    early_rows = up_to(7 * width, step)
    late_share = jax.ShapeDtypeStruct((late_rows // size_y, width), f32)
    early_share = jax.ShapeDtypeStruct((early_rows // size_y, width), f32)
    share_y = jax.ShapeDtypeStruct(((late_rows + early_rows) // size_y, width), f32)
    share_z = jax.ShapeDtypeStruct((share_y.shape[0] // size_z, width), f32)
    me_y = lax.axis_index("gy").reshape(1)
    me_z = lax.axis_index("gz").reshape(1)
    geo_rows = up_to(blocks + 1, GROUP) * SLOTS
    shared = [
        pltpu.VMEM((TILE, up_to(ext, LANES)), f32),
        pltpu.VMEM((geo_rows, LANES), jnp.int32),
        pltpu.VMEM((3 * geo_rows, LANES), f32),
    ]
    inner_sums = pl.pallas_call(
        functools.partial(inner_kernel, slots),
        in_specs=[smem] * 2 + [vmem] * 10,
        out_shape=jax.ShapeDtypeStruct((owned * TILE, LANES), f32),
        scratch_shapes=[
            pltpu.VMEM((owned * TILE, LANES), f32),
            pltpu.VMEM((LANES // TILE, slots * TILE * STEP, LANES), f32),
            pltpu.VMEM((TILE, blocks * LANES), f32),
            pltpu.VMEM((inner_rows, LANES), jnp.int32),
            pltpu.VMEM((3 * inner_rows, LANES), f32),
            pltpu.VMEM((ORDER_ROWS * inner_rows, LANES), f32),
            pltpu.VMEM((6 * inner_rows, LANES), f32),
            pltpu.VMEM((4 * ORDER_ROWS, wide), f32),
            pltpu.VMEM((4 * ORDER_ROWS, wide), bf16),
        ],
        compiler_params=pltpu.CompilerParams(vmem_limit_bytes=24 * MIB),
        cost_estimate=work(rows, 2 * geo_rows * LANES * 4 * ORDER_ROWS * wide * 3),
        name="edges_inner",
    )(
        flat_table,
        targets,
        rows,
        place,
        table,
        target_place,
        message_inner,
        b1,
        message_outer,
        b2,
        radial_weight,
        br,
    )
    out_s, out_v, grad, bias, *tables = pl.pallas_call(
        functools.partial(
            forward_kernel, tuple(halo), shapes, slots, hub_slots, chunk, size_y
        ),
        in_specs=[smem] * 6 + [vmem] * (20 + len(arrived)),
        out_shape=(
            jax.ShapeDtypeStruct((owned, width), bf16),
            jax.ShapeDtypeStruct((owned, 3 * width), bf16),
            jax.ShapeDtypeStruct((owned * TILE, width), f32),
            jax.ShapeDtypeStruct((TILE, width), f32),
            jax.ShapeDtypeStruct((ext_tiles, LANES), f32),
            jax.ShapeDtypeStruct((ORDER_ROWS * geo_rows, LANES), f32),
            jax.ShapeDtypeStruct((ORDER_ROWS * geo_rows, LANES), f32),
            jax.ShapeDtypeStruct((6 * geo_rows, LANES), f32),
        )
        + (early_share,) * size_y,
        scratch_shapes=[
            pltpu.VMEM((LANES // TILE, slots * TILE * STEP, LANES), f32),
            pltpu.VMEM((owned * TILE, LANES), f32),
        ]
        + shared
        + [
            pltpu.VMEM((4 * ORDER_ROWS, wide), f32),
            pltpu.VMEM((4 * ORDER_ROWS, wide), bf16),
            pltpu.VMEM((width, 2 * width), bf16),
            pltpu.VMEM((owned, 4 * width), f32),
            pltpu.VMEM((early_rows, width), f32),
        ],
        compiler_params=pltpu.CompilerParams(vmem_limit_bytes=24 * MIB),
        name="edges_forward",
    )(
        flat_table,
        flat_hub_table,
        targets,
        hub_atoms,
        hub_count,
        me_y,
        rows,
        place,
        cots,
        table,
        target_place,
        hub_table,
        hub_row,
        inner_sums,
        message_inner,
        b1,
        message_outer,
        b2,
        radial_weight,
        br,
        update_left,
        update_right,
        update_inner,
        b3,
        update_outer,
        b4,
        *arrived,
    )
    tables, early = tables[:4], rotated("gy", tables[4:])
    results = pl.pallas_call(
        functools.partial(backward_kernel, tuple(halo), shapes, slots, hub_slots),
        in_specs=[smem] * 5 + [vmem] * (12 + len(arrived)),
        out_shape=(
            jax.ShapeDtypeStruct((ext_tiles, LANES), f32),
            jax.ShapeDtypeStruct((blocks + 1, TILE, LANES), f32),
            jax.ShapeDtypeStruct((late_rows, width), f32),
        )
        + tuple(
            jax.ShapeDtypeStruct((packed_rows(count), 4 * width), f32)
            for count in (counts[0], counts[0], counts[1], counts[1])
        )
        + tuple(packet_shapes("gz", counts[2], 4 * width, 0)),
        scratch_shapes=[
            pltpu.VMEM((LANES // TILE, slots * TILE * STEP, LANES), f32),
            pltpu.VMEM((4 * ORDER_ROWS, wide), f32),
            pltpu.VMEM((4 * ORDER_ROWS, wide), bf16),
            pltpu.VMEM((slots * LANES, 4 * ORDER_ROWS), bf16),
            pltpu.VMEM((4 * ORDER_ROWS, slots * LANES), bf16),
            pltpu.VMEM((slots * LANES, wide), bf16),
            pltpu.VMEM((5 * TILE * SLOTS, LANES), f32),
            pltpu.VMEM((LANES, LANES), f32),
            pltpu.VMEM((4 * ORDER_ROWS, wide), f32),
        ],
        compiler_params=pltpu.CompilerParams(vmem_limit_bytes=22 * MIB),
        cost_estimate=work(rows, 2 * geo_rows * LANES * 4 * ORDER_ROWS * wide * 12),
        name="edges_backward",
    )(
        flat_table,
        flat_hub_table,
        targets,
        hub_atoms,
        hub_count,
        grad,
        bias,
        *tables,
        message_inner,
        b1,
        message_outer,
        b2,
        radial_weight,
        br,
        *arrived,
    )
    sums, target, late = results[:3]
    sides = results[3:7]
    packets, early = lax.optimization_barrier((results[7:], early))
    back_z = exchange("gz", packets)
    own, place, early, *late = pl.pallas_call(
        functools.partial(own_back_kernel, size_y),
        in_specs=[smem] + [vmem] * (12 + size_y),
        out_shape=(
            jax.ShapeDtypeStruct((owned, 4 * width), f32),
            jax.ShapeDtypeStruct((TILE, owned), f32),
            early_share,
        )
        + (late_share,) * size_y,
        scratch_shapes=[pltpu.VMEM((late_rows, width), f32)],
        compiler_params=pltpu.CompilerParams(vmem_limit_bytes=14 * MIB),
        name="own_backward",
    )(me_y, sums, target, late, scalar_feat, vector_feat, grad, names, hub_row, message_inner, b1, message_outer, b2, *early)
    ranges = [(h[0], h[1]) for h in halo]

    late = rotated("gy", late)
    results = pl.pallas_call(
        functools.partial(return_y_kernel, tuple(ranges[2:4]), (size_z, size_y)),
        in_specs=[smem] + [vmem] * (1 + shapes[2] + size_y + 3),
        out_shape=tuple(packet_shapes("gy", counts[1], 4 * width, 0)) + (share_z,) * size_z,
        scratch_shapes=[pltpu.VMEM(share_y.shape, f32)],
        compiler_params=middle,
        name="return_y",
    )(me_z, lists[2], *back_z, *late, early, *sides[2:4])
    packets, shares = results[: shapes[1]], results[shapes[1] :]

    shares = rotated("gz", shares)
    back_y = exchange("gy", packets)
    results = pl.pallas_call(
        functools.partial(return_x_kernel, tuple(ranges[0:2]), (size_z, size_y)),
        out_shape=tuple(packet_shapes("gx", counts[0], 4 * width, 0)) + (share_z,),
        compiler_params=middle,
        name="return_x",
    )(lists[2], lists[1], *back_z, *back_y, *shares, *sides[0:2])
    packets, keep = results[:-1], results[-1]

    shares = rotated("gx", [keep] * size_x)
    total = pl.pallas_call(
        sum_kernel, out_shape=share_z, compiler_params=small, name="sum_last"
    )(*shares)
    packets, total = lax.optimization_barrier((packets, total))
    shares = rotated("gz", [total] * size_z)
    back_x = exchange("gx", packets)
    own, place = pl.pallas_call(
        functools.partial(own_kernel, (shapes[2], shapes[1])),
        out_shape=(
            jax.ShapeDtypeStruct(own.shape, f32),
            jax.ShapeDtypeStruct(place.shape, f32),
        ),
        compiler_params=middle,
        cost_estimate=work(own, 2 * owned * 4 * width * 1056),
        name="own_partial",
    )(lists[2], lists[1], *back_z, *back_y, own, place)
    total = pl.pallas_call(
        join_kernel,
        in_specs=[smem] + [vmem] * size_z,
        out_shape=share_y,
        compiler_params=small,
        name="join_shares",
    )(me_z, *shares)
    total, own, place = lax.optimization_barrier((total, own, place))
    shares = gathered("gy", total)
    scalar_grad, vector_grad, positions_grad = pl.pallas_call(
        functools.partial(own_kernel, (shapes[0],)),
        out_shape=(
            jax.ShapeDtypeStruct((owned, width), f32),
            jax.ShapeDtypeStruct((owned, 3 * width), f32),
            jax.ShapeDtypeStruct((3, owned), f32),
        ),
        compiler_params=middle,
        cost_estimate=work(own, 2 * owned * 4 * width * 400),
        name="own_last",
    )(lists[0], *back_x, own, place)

    def like(x):
        return jax.ShapeDtypeStruct(x.shape, f32)

    weights = pl.pallas_call(
        functools.partial(unpack_kernel, (size_y, size_z), late_share.shape[0]),
        in_specs=[smem] + [vmem] * size_y,
        out_shape=tuple(
            like(x)
            for x in (
                message_inner,
                message_inner_bias,
                message_outer,
                message_outer_bias,
                radial_weight,
                radial_bias,
                update_left,
                update_right,
                update_inner,
                update_inner_bias,
                update_outer,
                update_outer_bias,
            )
        ),
        scratch_shapes=[
            pltpu.VMEM((late_rows, width), f32),
            pltpu.VMEM((early_rows, width), f32),
            pltpu.VMEM((late_rows + early_rows, width), f32),
        ],
        compiler_params=small,
        name="unpack_weights",
    )(me_y, *shares)
    return (out_s, out_v, scalar_grad, vector_grad, positions_grad, *weights)


def solution(mesh):
    cells = P(("gx", "gy", "gz"), None)
    columns = P(None, ("gx", "gy", "gz"))
    faces = P(("gx", "gy", "gz"), None, None)
    flat = P(("gx", "gy", "gz"))
    return jax.shard_map(
        local,
        mesh=mesh,
        in_specs=(cells, cells, columns)
        + (P(),) * 12
        + (cells, cells, faces, faces, faces, columns, flat, columns, flat),
        out_specs=(cells, cells, cells, cells, columns) + (P(),) * 12,
        check_vma=False,
    )
```
